128 devices in a mesh: ctx: 32 (over y_lo, x, z), ch: 4 (over y_hi, core).
Axes of the slice: x: 4, y: 4 (y_hi: 2, y_lo: 2; y = y_hi * 2 + y_lo), z: 4, core: 2. Of those that a mesh axis runs over, the one named last changes fastest.
Arguments:
- inputs: bfloat16 [1, 4096, 8192], P(None, 'ch', 'ctx'), may hold values from -0.078125 to 0.078125
- grad_out: bfloat16 [1, 4096, 8192], P(None, 'ch', 'ctx'), may hold values from -6 to 6
- filters: bfloat16 [1024, 8192], P(None, 'ctx'), may hold values from -0.0625 to 0.0625
Outputs:
- dinputs: bfloat16 [1, 4096, 8192], P(None, 'ch', 'ctx')
- dfilters: float32 [1024, 8192], P(None, ('ctx', 'ch'))
The draws below stay inside these ranges and needn't reach their ends.
All inputs are finite; a program needn't handle non-finite values.
Results may differ from the reference program's by a relative error of at most 0.011.
Values may be sent and summed in bfloat16 or wider, within the bound.
No kernel may reach another device: no remote copies, remote signals or barrier semaphores. Data moves between devices by JAX's collectives and lax.ppermute only.
A program may use at most 128 MiB of HBM per device.

```python
import jax
import jax.numpy as jnp
from jax import lax

CHANS = 4096
FILTERS = 1024
SEQS = 1
L = 8192


def steps_of(own_key, shape, shards, least, top_value):
    def one(position, blocks):
        draws = jax.random.uniform(jax.random.fold_in(jax.random.fold_in(own_key, 6), position), (blocks,), jnp.float32, least / len(shards), top_value / len(shards))
        return jnp.repeat(jnp.exp(draws), shape[position] // blocks).reshape((-1,) + (1,) * (len(shape) - position - 1))

    gain = one(*shards[0])
    for cut in shards[1:]:
        gain = gain * one(*cut)
    return gain


def scatter_about(stream_key, shape, width, most, cuts=(), kind=jnp.bfloat16):
    result = jax.random.normal(stream_key, shape, jnp.float32) * width
    if len(cuts) > 0:
        result = steps_of(stream_key, shape, cuts, -0.22, 0.18) * result
    return jnp.clip(result, min=-most, max=most).astype(kind)


def setup_inputs(seed: int = 0) -> dict:
    splits = jax.random.split(jax.random.key(seed), 4)
    return {
        "inputs": scatter_about(splits[0], (SEQS, CHANS, L), ((CHANS // FILTERS * SEQS * L) ** -0.5), 0.078125, ((1, 4), (2, 32))),
        "grad_out": scatter_about(splits[1], (SEQS, CHANS, L), 1.0, 6.0, ((1, 4), (2, 32))),
        "filters": scatter_about(splits[2], (FILTERS, L), L ** -0.5, 0.0625, ((1, 32),)),
    }


def reference(inputs, grad_out, filters):
    length_seq = inputs.shape[2]
    points = 2 * length_seq
    groups = inputs.shape[1] // filters.shape[0]
    spec_filter = jnp.fft.rfft(filters.astype(jnp.float32), n=points)
    filter_chan = jnp.tile(spec_filter, (groups, 1))

    def step(carry, operands):
        seq_in, seq_grad = operands
        spec_in = jnp.fft.rfft(seq_in.astype(jnp.float32), n=points)
        spec_grad = jnp.fft.rfft(seq_grad.astype(jnp.float32), n=points)
        backed = jnp.fft.irfft(jnp.conj(filter_chan) * spec_grad, n=points)[:, :length_seq]
        cross = jnp.conj(spec_in) * spec_grad
        return (carry[0] + jnp.real(cross), carry[1] + jnp.imag(cross)), backed.astype(jnp.bfloat16)

    zeros_init = jnp.zeros((inputs.shape[1], points // 2 + 1), jnp.float32)
    (cross_re, cross_im), dinputs = lax.scan(step, (zeros_init, zeros_init), (inputs, grad_out))
    summed = lax.complex(cross_re, cross_im).reshape(groups, filters.shape[0], -1).sum(0)
    dfilters = jnp.fft.irfft(summed, n=points)[:, :length_seq]
    return dinputs, dfilters
```

```python
import math

import jax
import jax.numpy as jnp
import ml_dtypes
import numpy as np
from jax import lax
from jax.experimental import pallas as pl
from jax.experimental.pallas import tpu as pltpu
from jax.sharding import PartitionSpec as P

BF16 = jnp.bfloat16
F32 = jnp.float32
GROUP = 8
HALF = 128
ROWS_OUT = 24


def halves(table):
    high = table.astype(ml_dtypes.bfloat16)
    low = (table - high.astype(np.float64)).astype(ml_dtypes.bfloat16)
    return high, low


def make_tables(n_lead, n_trail):
    points = n_lead * n_trail
    shifted = np.arange(n_lead)[:, None] + 0.25
    angle = 2.0 * math.pi / n_lead * shifted * np.arange(n_lead)[None, :]
    eye = np.eye(GROUP)
    lead = np.concatenate([np.kron(np.cos(angle), eye), np.kron(-np.sin(angle), eye)], 0)
    turn = 2.0 * math.pi / points * shifted * np.arange(n_trail)[None, :]
    turn = np.repeat(turn, GROUP, axis=0)
    twist = np.stack([np.cos(turn), -np.sin(turn)]).astype(np.float32)
    angle = 2.0 * math.pi / n_trail * (np.arange(n_trail)[:, None] * np.arange(n_trail)[None, :] % n_trail)
    cos, sin = np.cos(angle), np.sin(angle)
    trail = np.block([[cos, -sin], [sin, cos]])
    lead_back = np.concatenate(halves(lead.T), 1)
    return np.concatenate(halves(lead), 1), lead_back, np.stack(halves(trail)), twist


def dot(left, right):
    return jnp.dot(left, right, preferred_element_type=F32)


def pack_kernel(half_ref, in_ref, grad_ref, filt_ref, out_ref):
    del half_ref
    for base, ref in ((0, in_ref), (2 * GROUP, grad_ref)):
        values = ref[...].astype(F32)
        left = values[:, :HALF].reshape(-1, GROUP, HALF)
        right = values[:, HALF:].reshape(-1, GROUP, HALF)
        out_ref[:, base : base + 2 * GROUP, :] = jnp.concatenate([left, right], 1).astype(BF16)
    values = filt_ref[...].astype(F32).reshape(-1, GROUP, HALF)
    out_ref[:, 4 * GROUP :, :] = values.astype(BF16)


def pack(inputs, grad_out, filters, half):
    rows, width = inputs.shape
    tile = rows // 4
    grid_spec = pltpu.PrefetchScalarGridSpec(
        num_scalar_prefetch=1,
        grid=(rows // tile,),
        in_specs=[
            pl.BlockSpec((tile, width), lambda s, h: (s, 0)),
            pl.BlockSpec((tile, width), lambda s, h: (s, 0)),
            pl.BlockSpec((tile, HALF), lambda s, h: (s, h[0])),
        ],
        out_specs=pl.BlockSpec((tile // GROUP, 5 * GROUP, HALF), lambda s, h: (s, 0, 0)),
    )
    return pl.pallas_call(
        pack_kernel,
        grid_spec=grid_spec,
        out_shape=jax.ShapeDtypeStruct((rows // GROUP, 5 * GROUP, HALF), BF16),
        name="pack",
    )(half, inputs, grad_out, filters)


def split(values):
    high = values.astype(BF16)
    return high, (values - high.astype(F32)).astype(BF16)


def twisted(real, imag, tw_re, tw_im):
    return real * tw_re - imag * tw_im, real * tw_im + imag * tw_re


def unit_kernel(recv_ref, lead_ref, back_ref, trail_ref, twist_ref, out_ref, filt_spec, cross):
    n_lead = recv_ref.shape[0]
    n_slab = recv_ref.shape[1]
    rows = n_lead * GROUP
    width = 2 * HALF
    scale = 1.0 / (n_lead * width)
    trail_high, trail_low = trail_ref[0], trail_ref[1]

    def sequences(block):
        left = block[:, :GROUP].reshape(rows, HALF)
        right = block[:, GROUP:].reshape(rows, HALF)
        return jnp.concatenate([left, right], 1).astype(BF16)

    def lead(values):
        return dot(lead_ref[...], jnp.concatenate([values, values], 0))

    def precise(values):
        high, low = split(values)
        return dot(high, trail_high) + dot(low, trail_high) + dot(high, trail_low)

    def quick(values):
        high = values.astype(BF16)
        return dot(high, trail_high) + dot(high, trail_low)

    def turn(first):
        real, imag = twisted(first[:rows], first[rows:], twist_ref[0], twist_ref[1])
        return jnp.concatenate([real, imag], 1)

    def turn_back(second):
        imag, real = second[:, :width], second[:, width:]
        tw_re, tw_im = twist_ref[0], -twist_ref[1]
        real, imag = twisted(real, imag, tw_re, tw_im)
        return jnp.concatenate([real, imag], 0)

    filt = jnp.concatenate(
        [recv_ref[:, h, 4 * GROUP :, :].astype(F32).reshape(rows, HALF) for h in (0, 1)], 1
    ).astype(BF16)
    filt_spec[...] = precise(turn(lead(filt)))
    cross[...] = jnp.zeros_like(cross)

    def one_slab(slab, unused):
        block = recv_ref[:, slab, : 4 * GROUP, :].astype(F32)
        seq_in = sequences(block[:, : 2 * GROUP])
        seq_grad = sequences(block[:, 2 * GROUP :])
        spec_in = quick(turn(lead(seq_in)))
        spec_grad = quick(turn(lead(seq_grad)))
        in_re, in_im = spec_in[:, :width], spec_in[:, width:]
        grad_re, grad_im = spec_grad[:, :width], spec_grad[:, width:]
        cross[:, :width] += in_re * grad_im - in_im * grad_re
        cross[:, width:] += in_re * grad_re + in_im * grad_im
        filt_re, filt_im = filt_spec[:, :width], filt_spec[:, width:]
        back_re = filt_re * grad_re + filt_im * grad_im
        back_im = filt_re * grad_im - filt_im * grad_re
        turned = turn_back(quick(jnp.concatenate([back_im, back_re], 1))).astype(BF16)
        result = dot(back_ref[...], jnp.concatenate([turned, turned], 0)) * scale
        left = result[:, :HALF].reshape(n_lead, GROUP, HALF)
        right = result[:, HALF:].reshape(n_lead, GROUP, HALF)
        out_ref[:, slab, : 2 * GROUP, :] = jnp.concatenate([left, right], 1).astype(BF16)
        return unused

    lax.fori_loop(0, n_slab, one_slab, 0)

    high, low = split(turn_back(precise(cross[...])))
    table = back_ref[...]
    result = dot(table, jnp.concatenate([high, high], 0)) + dot(table[:, : 2 * rows], low)
    result = result * scale
    lane = lax.broadcasted_iota(jnp.int32, (rows, HALF), 1)
    quarter = HALF // 2
    for h in (0, 1):
        part = result[:, h * HALF : (h + 1) * HALF]
        high = part.astype(BF16).astype(F32)
        low = part - high
        even = jnp.where(lane < quarter, high, pltpu.roll(low, quarter, 1))
        odd = jnp.where(lane < quarter, pltpu.roll(high, quarter, 1), low)
        for q, both in ((0, even), (1, odd)):
            out_ref[:, 2 * h + q, 2 * GROUP :, :] = both.reshape(n_lead, GROUP, HALF).astype(BF16)


def unit(received, n_lead, n_slab):
    tables = make_tables(n_lead, 2 * HALF)
    rows = n_lead * GROUP
    received = received.reshape(n_lead, n_slab, 5 * GROUP, HALF)
    vmem = pl.BlockSpec(memory_space=pltpu.VMEM)
    out = pl.pallas_call(
        unit_kernel,
        in_specs=[vmem] * 5,
        out_specs=vmem,
        out_shape=jax.ShapeDtypeStruct((n_lead, n_slab, ROWS_OUT, HALF), BF16),
        scratch_shapes=[pltpu.VMEM((rows, 4 * HALF), F32), pltpu.VMEM((rows, 4 * HALF), F32)],
        compiler_params=pltpu.CompilerParams(vmem_limit_bytes=40 * 2**20),
        name="unit",
    )(received, *[jnp.asarray(t) for t in tables])
    return out.reshape(n_lead * n_slab, ROWS_OUT, HALF)


def unpack_kernel(recv_ref, pick_ref, din_ref, dfilt_ref):
    values = recv_ref[...].astype(F32)
    count = values.shape[0]
    left = values[:, :GROUP].reshape(count * GROUP, HALF)
    right = values[:, GROUP : 2 * GROUP].reshape(count * GROUP, HALF)
    din_ref[...] = jnp.concatenate([left, right], 1).astype(BF16)
    both = values[:, 2 * GROUP :].reshape(count * GROUP, HALF).astype(BF16)
    dfilt_ref[...] = lax.dot_general(
        pick_ref[...], both, (((1,), (1,)), ((), ())), preferred_element_type=F32
    )


def unpack(received):
    count = received.shape[0]
    quarter = HALF // 2
    pick = np.concatenate([np.eye(quarter), np.eye(quarter)], 1).astype(ml_dtypes.bfloat16)
    steps = 4
    tile = count // steps
    return pl.pallas_call(
        unpack_kernel,
        grid=(steps,),
        in_specs=[
            pl.BlockSpec((tile, ROWS_OUT, HALF), lambda s: (s, 0, 0)),
            pl.BlockSpec((quarter, HALF), lambda s: (0, 0)),
        ],
        out_specs=[
            pl.BlockSpec((tile * GROUP, 2 * HALF), lambda s: (s, 0)),
            pl.BlockSpec((quarter, tile * GROUP), lambda s: (0, s)),
        ],
        out_shape=[
            jax.ShapeDtypeStruct((count * GROUP, 2 * HALF), BF16),
            jax.ShapeDtypeStruct((quarter, count * GROUP), F32),
        ],
        name="unpack",
    )(received, jnp.asarray(pick))


def per_device(inputs, grad_out, filters):
    n_ctx, n_ch = lax.axis_size("ctx"), lax.axis_size("ch")
    half = (lax.axis_index("ch") % 2).astype(jnp.int32).reshape(1)
    packed = pack(inputs[0], grad_out[0], filters, half)
    received = lax.all_to_all(packed, ("ctx", "ch"), split_axis=0, concat_axis=0)
    returned = unit(received, n_ctx, n_ch)
    returned = lax.all_to_all(returned, ("ctx", "ch"), split_axis=0, concat_axis=0)
    dinputs, dfilters = unpack(returned)
    return dinputs[None], dfilters.T


def solution(mesh):
    placed = (P(None, "ch", "ctx"), P(None, "ch", "ctx"), P(None, "ctx"))
    return jax.shard_map(
        per_device,
        mesh=mesh,
        in_specs=placed,
        out_specs=(P(None, "ch", "ctx"), P(None, ("ctx", "ch"))),
        check_vma=False,
    )
```

```python
import functools
import math

import jax
import jax.numpy as jnp
import ml_dtypes
import numpy as np
from jax import lax
from jax.experimental import pallas as pl
from jax.experimental.pallas import tpu as pltpu
from jax.sharding import PartitionSpec as P

BF16 = jnp.bfloat16
F32 = jnp.float32
GROUP = 8
HALF = 128
WIDTH = 2 * HALF


def halves(table):
    high = table.astype(ml_dtypes.bfloat16)
    low = (table - high.astype(np.float64)).astype(ml_dtypes.bfloat16)
    return np.stack([high, low])


def scaled(table):
    sizes, counts = np.unique(np.round(np.abs(table), 12), return_counts=True)

    def loss(factor):
        rounded = (sizes * factor).astype(ml_dtypes.bfloat16).astype(np.float64) / factor
        return np.sum(counts * (rounded - sizes) ** 2)

    factor = min(np.linspace(1.0, 2.0, 1025)[:-1], key=loss)
    return table * factor, float(factor)


def make_tables(n_lead):
    points = n_lead * WIDTH
    shifted = np.arange(n_lead)[:, None] + 0.25
    angle = 2.0 * math.pi / n_lead * shifted * np.arange(n_lead)[None, :]
    lead, lead_factor = scaled(np.concatenate([np.cos(angle), -np.sin(angle)], 0))
    lead = np.kron(lead, np.eye(GROUP))
    turn = 2.0 * math.pi / points * shifted * np.arange(WIDTH)[None, :]
    turn = np.repeat(turn, GROUP, axis=0)
    twist = np.stack([np.cos(turn), -np.sin(turn)]).astype(np.float32)
    angle = 2.0 * math.pi / WIDTH * (np.arange(WIDTH)[:, None] * np.arange(WIDTH)[None, :] % WIDTH)
    cos, sin = np.cos(angle), np.sin(angle)
    trail, trail_factor = scaled(np.block([[cos, -sin], [sin, cos]]))
    undo = 1.0 / (points * (lead_factor * trail_factor) ** 3)
    return halves(lead), halves(lead.T), halves(trail), twist, undo


def dot(left, right):
    return jnp.dot(left, right, preferred_element_type=F32)


def split(values):
    high = values.astype(BF16)
    return high, (values - high.astype(F32)).astype(BF16)


def pack_kernel(in_ref, grad_ref, filt_ref, out_ref, sems):
    half = lax.axis_index("ch") % 2
    copies = [
        pltpu.make_async_copy(in_ref, out_ref.at[:, 0:2], sems.at[0]),
        pltpu.make_async_copy(grad_ref, out_ref.at[:, 2:4], sems.at[1]),
        pltpu.make_async_copy(filt_ref.at[:, half], out_ref.at[:, 4], sems.at[2]),
    ]
    for copy in copies:
        copy.start()
    for copy in copies:
        copy.wait()


def pack(inputs, grad_out, filters):
    def tiles(values):
        return values.reshape(-1, GROUP, 2, HALF).transpose(0, 2, 1, 3)

    parts = [tiles(values) for values in (inputs, grad_out, filters)]
    anywhere = pl.BlockSpec(memory_space=pl.ANY)
    return pl.pallas_call(
        pack_kernel,
        in_specs=[anywhere] * 3,
        out_specs=anywhere,
        out_shape=jax.ShapeDtypeStruct((parts[0].shape[0], 5, GROUP, HALF), BF16),
        scratch_shapes=[pltpu.SemaphoreType.DMA((3,))],
        name="pack",
    )(*parts)


def unit_kernel(undo, recv_ref, lead_ref, back_ref, trail_ref, twist_ref, out_ref, filt_spec, cross):
    n_lead, n_slab = recv_ref.shape[:2]
    rows = n_lead * GROUP

    def sequences(first, second):
        parts = [part.astype(F32).reshape(rows, HALF) for part in (first, second)]
        return jnp.concatenate(parts, 1).astype(BF16)

    def turn(first):
        real, imag = first[:rows], first[rows:]
        tw_re, tw_im = twist_ref[0], twist_ref[1]
        return jnp.concatenate([real * tw_re - imag * tw_im, real * tw_im + imag * tw_re], 1)

    def turn_back(second):
        imag, real = second[:, :WIDTH], second[:, WIDTH:]
        tw_re, tw_im = twist_ref[0], twist_ref[1]
        return jnp.concatenate([real * tw_re + imag * tw_im, imag * tw_re - real * tw_im], 0)

    def precise(values):
        high, low = split(values)
        return dot(high, trail_ref[0]) + dot(low, trail_ref[0]) + dot(high, trail_ref[1])

    def spectrum(values):
        return dot(turn(dot(lead_ref[0], values)).astype(BF16), trail_ref[0])

    def forward(slab):
        spec_in = spectrum(sequences(recv_ref[:, slab, 0], recv_ref[:, slab, 1]))
        spec_grad = spectrum(sequences(recv_ref[:, slab, 2], recv_ref[:, slab, 3]))
        return spec_in, spec_grad

    def backward(slab, spec_in, spec_grad):
        in_re, in_im = spec_in[:, :WIDTH], spec_in[:, WIDTH:]
        grad_re, grad_im = spec_grad[:, :WIDTH], spec_grad[:, WIDTH:]
        cross_im = in_re * grad_im - in_im * grad_re
        cross_re = in_re * grad_re + in_im * grad_im
        if slab == 0:
            cross[:, :WIDTH] = cross_im
            cross[:, WIDTH:] = cross_re
        else:
            cross[:, :WIDTH] += cross_im
            cross[:, WIDTH:] += cross_re
        filt_re, filt_im = filt_spec[:, :WIDTH], filt_spec[:, WIDTH:]
        back_re = filt_re * grad_re + filt_im * grad_im
        back_im = filt_re * grad_im - filt_im * grad_re
        product = jnp.concatenate([back_im, back_re], 1).astype(BF16)
        turned = turn_back(dot(product, trail_ref[0])).astype(BF16)
        result = dot(back_ref[0], turned) * undo
        for h in (0, 1):
            part = result[:, h * HALF : (h + 1) * HALF].reshape(n_lead, GROUP, HALF)
            out_ref[:, slab, h] = part.astype(BF16)

    filt = sequences(recv_ref[:, 0, 4], recv_ref[:, 1, 4])
    filt_spec[...] = precise(turn(dot(lead_ref[0], filt) + dot(lead_ref[1], filt)))

    ahead = forward(0)
    for slab in range(n_slab):
        here = ahead
        if slab + 1 < n_slab:
            ahead = forward(slab + 1)
        backward(slab, *here)

    high, low = split(turn_back(precise(cross[...])))
    result = (dot(back_ref[0], high) + dot(back_ref[0], low) + dot(back_ref[1], high)) * undo
    lane = lax.broadcasted_iota(jnp.int32, (rows, HALF), 1)
    quarter = HALF // 2
    for h in (0, 1):
        part = result[:, h * HALF : (h + 1) * HALF]
        high = part.astype(BF16).astype(F32)
        low = part - high
        even = jnp.where(lane < quarter, high, pltpu.roll(low, quarter, 1))
        odd = jnp.where(lane < quarter, pltpu.roll(high, quarter, 1), low)
        for q, both in ((0, even), (1, odd)):
            out_ref[:, 2 * h + q, 2] = both.reshape(n_lead, GROUP, HALF).astype(BF16)


def unit(received, n_lead, n_slab):
    *tables, undo = make_tables(n_lead)
    spectra = pltpu.VMEM((n_lead * GROUP, 2 * WIDTH), F32)
    vmem = pl.BlockSpec(memory_space=pltpu.VMEM)
    out = pl.pallas_call(
        functools.partial(unit_kernel, undo),
        in_specs=[vmem] * 5,
        out_specs=vmem,
        out_shape=jax.ShapeDtypeStruct((n_lead, n_slab, 3, GROUP, HALF), BF16),
        scratch_shapes=[spectra, spectra],
        compiler_params=pltpu.CompilerParams(vmem_limit_bytes=40 * 2**20),
        name="unit",
    )(received.reshape(n_lead, n_slab, 5, GROUP, HALF), *[jnp.asarray(t) for t in tables])
    return out.reshape(n_lead * n_slab, 3, GROUP, HALF)


def unpack_kernel(recv_ref, pick_ref, din_ref, dfilt_ref, staged, sems):
    copy = pltpu.make_async_copy(recv_ref.at[:, 0:2], din_ref, sems.at[0])
    copy.start()
    both = recv_ref[:, 2].astype(F32).reshape(-1, HALF).astype(BF16)
    staged[...] = lax.dot_general(
        pick_ref[...], both, (((1,), (1,)), ((), ())), preferred_element_type=F32
    )
    other = pltpu.make_async_copy(staged, dfilt_ref, sems.at[1])
    other.start()
    copy.wait()
    other.wait()


def unpack(received):
    count = received.shape[0]
    quarter = HALF // 2
    pick = np.concatenate([np.eye(quarter), np.eye(quarter)], 1).astype(ml_dtypes.bfloat16)
    vmem, anywhere = pl.BlockSpec(memory_space=pltpu.VMEM), pl.BlockSpec(memory_space=pl.ANY)
    dinputs, dfilters = pl.pallas_call(
        unpack_kernel,
        in_specs=[vmem, vmem],
        out_specs=[anywhere, anywhere],
        out_shape=[
            jax.ShapeDtypeStruct((count, 2, GROUP, HALF), BF16),
            jax.ShapeDtypeStruct((quarter, count * GROUP), F32),
        ],
        scratch_shapes=[pltpu.VMEM((quarter, count * GROUP), F32), pltpu.SemaphoreType.DMA((2,))],
        name="unpack",
    )(received, jnp.asarray(pick))
    return dinputs.transpose(0, 2, 1, 3).reshape(count * GROUP, WIDTH), dfilters.T


def per_device(inputs, grad_out, filters):
    n_ctx, n_ch = lax.axis_size("ctx"), lax.axis_size("ch")

    def exchange(blocks):
        return lax.all_to_all(blocks, ("ctx", "ch"), split_axis=0, concat_axis=0)

    received = exchange(pack(inputs[0], grad_out[0], filters))
    dinputs, dfilters = unpack(exchange(unit(received, n_ctx, n_ch)))
    return dinputs[None], dfilters


def solution(mesh):
    placed = (P(None, "ch", "ctx"), P(None, "ch", "ctx"), P(None, "ctx"))
    return jax.shard_map(
        per_device,
        mesh=mesh,
        in_specs=placed,
        out_specs=(P(None, "ch", "ctx"), P(None, ("ctx", "ch"))),
        check_vma=False,
    )
```

```python
import functools
import math

import jax
import jax.numpy as jnp
import ml_dtypes
import numpy as np
from jax import lax
from jax.experimental import pallas as pl
from jax.experimental.pallas import tpu as pltpu
from jax.sharding import PartitionSpec as P

BF16 = jnp.bfloat16
F32 = jnp.float32
GROUP = 8
HALF = 128
WIDTH = 2 * HALF


def halves(table):
    high = table.astype(ml_dtypes.bfloat16)
    low = (table - high.astype(np.float64)).astype(ml_dtypes.bfloat16)
    return np.stack([high, low])


def scaled(table):
    sizes, counts = np.unique(np.round(np.abs(table), 12), return_counts=True)

    def loss(factor):
        rounded = (sizes * factor).astype(ml_dtypes.bfloat16).astype(np.float64) / factor
        return np.sum(counts * (rounded - sizes) ** 2)

    factor = min(np.linspace(1.0, 2.0, 1025)[:-1], key=loss)
    return table * factor, float(factor)


def make_tables(n_lead):
    points = n_lead * WIDTH
    shifted = np.arange(n_lead)[:, None] + 0.25
    angle = 2.0 * math.pi / n_lead * shifted * np.arange(n_lead)[None, :]
    lead, lead_factor = scaled(np.concatenate([np.cos(angle), -np.sin(angle)], 0))
    lead = np.kron(lead, np.eye(GROUP))
    turn = 2.0 * math.pi / points * shifted * np.arange(WIDTH)[None, :]
    turn = np.repeat(turn, GROUP, axis=0)
    twist = np.stack([np.cos(turn), -np.sin(turn)]).astype(np.float32)
    angle = 2.0 * math.pi / WIDTH * (np.arange(WIDTH)[:, None] * np.arange(WIDTH)[None, :] % WIDTH)
    cos, sin = np.cos(angle), np.sin(angle)
    trail, trail_factor = scaled(np.block([[cos, -sin], [sin, cos]]))
    undo = 1.0 / (points * (lead_factor * trail_factor) ** 3)
    return halves(lead), halves(lead.T), halves(trail), twist, undo


def dot(left, right):
    return jnp.dot(left, right, preferred_element_type=F32)


def split(values):
    high = values.astype(BF16)
    return high, (values - high.astype(F32)).astype(BF16)


def pack_kernel(in_ref, grad_ref, filt_ref, out_ref, sems):
    half = lax.axis_index("ch") % 2
    copies = [
        pltpu.make_async_copy(in_ref, out_ref.at[:, 0:2], sems.at[0]),
        pltpu.make_async_copy(grad_ref, out_ref.at[:, 2:4], sems.at[1]),
        pltpu.make_async_copy(filt_ref.at[:, half], out_ref.at[:, 4], sems.at[2]),
    ]
    for copy in copies:
        copy.start()
    for copy in copies:
        copy.wait()


def pack(inputs, grad_out, filters):
    def tiles(values):
        return values.reshape(-1, GROUP, 2, HALF).transpose(0, 2, 1, 3)

    parts = [tiles(values) for values in (inputs, grad_out, filters)]
    return pl.pallas_call(
        pack_kernel,
        in_specs=[pl.BlockSpec(memory_space=pl.ANY)] * 3,
        out_specs=pl.BlockSpec(memory_space=pltpu.VMEM),
        out_shape=jax.ShapeDtypeStruct((parts[0].shape[0], 5, GROUP, HALF), BF16),
        scratch_shapes=[pltpu.SemaphoreType.DMA((3,))],
        name="pack",
    )(*parts)


def unit_kernel(undo, recv_ref, lead_ref, back_ref, trail_ref, twist_ref, out_ref, filt_spec, cross):
    n_lead, n_slab = recv_ref.shape[:2]
    rows = n_lead * GROUP

    def sequences(first, second):
        parts = [part.astype(F32).reshape(rows, HALF) for part in (first, second)]
        return jnp.concatenate(parts, 1).astype(BF16)

    def turn(first):
        real, imag = first[:rows], first[rows:]
        tw_re, tw_im = twist_ref[0], twist_ref[1]
        return jnp.concatenate([real * tw_re - imag * tw_im, real * tw_im + imag * tw_re], 1)

    def turn_back(second):
        imag, real = second[:, :WIDTH], second[:, WIDTH:]
        tw_re, tw_im = twist_ref[0], twist_ref[1]
        return jnp.concatenate([real * tw_re + imag * tw_im, imag * tw_re - real * tw_im], 0)

    def precise(values):
        high, low = split(values)
        return dot(high, trail_ref[0]) + dot(low, trail_ref[0]) + dot(high, trail_ref[1])

    def spectrum(values):
        return dot(turn(dot(lead_ref[0], values)).astype(BF16), trail_ref[0])

    def forward(slab):
        spec_in = spectrum(sequences(recv_ref[:, slab, 0], recv_ref[:, slab, 1]))
        spec_grad = spectrum(sequences(recv_ref[:, slab, 2], recv_ref[:, slab, 3]))
        return spec_in, spec_grad

    def backward(slab, spec_in, spec_grad):
        in_re, in_im = spec_in[:, :WIDTH], spec_in[:, WIDTH:]
        grad_re, grad_im = spec_grad[:, :WIDTH], spec_grad[:, WIDTH:]
        cross_im = in_re * grad_im - in_im * grad_re
        cross_re = in_re * grad_re + in_im * grad_im
        if slab == 0:
            cross[:, :WIDTH] = cross_im
            cross[:, WIDTH:] = cross_re
        else:
            cross[:, :WIDTH] += cross_im
            cross[:, WIDTH:] += cross_re
        filt_re, filt_im = filt_spec[:, :WIDTH], filt_spec[:, WIDTH:]
        back_re = filt_re * grad_re + filt_im * grad_im
        back_im = filt_re * grad_im - filt_im * grad_re
        product = jnp.concatenate([back_im, back_re], 1).astype(BF16)
        turned = turn_back(dot(product, trail_ref[0])).astype(BF16)
        result = dot(back_ref[0], turned) * undo
        for h in (0, 1):
            part = result[:, h * HALF : (h + 1) * HALF].reshape(n_lead, GROUP, HALF)
            out_ref[:, slab, h] = part.astype(BF16)

    filt = sequences(recv_ref[:, 0, 4], recv_ref[:, 1, 4])
    filt_spec[...] = precise(turn(dot(lead_ref[0], filt) + dot(lead_ref[1], filt)))

    ahead = forward(0)
    for slab in range(n_slab):
        here = ahead
        if slab + 1 < n_slab:
            ahead = forward(slab + 1)
        backward(slab, *here)

    high, low = split(turn_back(precise(cross[...])))
    result = (dot(back_ref[0], high) + dot(back_ref[0], low) + dot(back_ref[1], high)) * undo
    lane = lax.broadcasted_iota(jnp.int32, (rows, HALF), 1)
    quarter = HALF // 2
    for h in (0, 1):
        part = result[:, h * HALF : (h + 1) * HALF]
        high = part.astype(BF16).astype(F32)
        low = part - high
        even = jnp.where(lane < quarter, high, pltpu.roll(low, quarter, 1))
        odd = jnp.where(lane < quarter, pltpu.roll(high, quarter, 1), low)
        for q, both in ((0, even), (1, odd)):
            out_ref[:, 2 * h + q, 2] = both.reshape(n_lead, GROUP, HALF).astype(BF16)


def unit(received, n_lead, n_slab):
    *tables, undo = make_tables(n_lead)
    spectra = pltpu.VMEM((n_lead * GROUP, 2 * WIDTH), F32)
    vmem = pl.BlockSpec(memory_space=pltpu.VMEM)
    out = pl.pallas_call(
        functools.partial(unit_kernel, undo),
        in_specs=[vmem] * 5,
        out_specs=vmem,
        out_shape=jax.ShapeDtypeStruct((n_lead, n_slab, 3, GROUP, HALF), BF16),
        scratch_shapes=[spectra, spectra],
        compiler_params=pltpu.CompilerParams(vmem_limit_bytes=40 * 2**20),
        name="unit",
    )(received.reshape(n_lead, n_slab, 5, GROUP, HALF), *[jnp.asarray(t) for t in tables])
    return out.reshape(n_lead * n_slab, 3, GROUP, HALF)


def unpack_kernel(recv_ref, pick_ref, din_ref, dfilt_ref, staged, sems):
    copy = pltpu.make_async_copy(recv_ref.at[:, 0:2], din_ref, sems.at[0])
    copy.start()
    both = recv_ref[:, 2].astype(F32).reshape(-1, HALF).astype(BF16)
    staged[...] = lax.dot_general(
        pick_ref[...], both, (((1,), (1,)), ((), ())), preferred_element_type=F32
    )
    other = pltpu.make_async_copy(staged, dfilt_ref, sems.at[1])
    other.start()
    copy.wait()
    other.wait()


def unpack(received):
    count = received.shape[0]
    quarter = HALF // 2
    pick = np.concatenate([np.eye(quarter), np.eye(quarter)], 1).astype(ml_dtypes.bfloat16)
    vmem, anywhere = pl.BlockSpec(memory_space=pltpu.VMEM), pl.BlockSpec(memory_space=pl.ANY)
    dinputs, dfilters = pl.pallas_call(
        unpack_kernel,
        in_specs=[vmem, vmem],
        out_specs=[anywhere, anywhere],
        out_shape=[
            jax.ShapeDtypeStruct((count, 2, GROUP, HALF), BF16),
            jax.ShapeDtypeStruct((quarter, count * GROUP), F32),
        ],
        scratch_shapes=[pltpu.VMEM((quarter, count * GROUP), F32), pltpu.SemaphoreType.DMA((2,))],
        name="unpack",
    )(received, jnp.asarray(pick))
    return dinputs.transpose(0, 2, 1, 3).reshape(count * GROUP, WIDTH), dfilters.T


def per_device(inputs, grad_out, filters):
    n_ctx, n_ch = lax.axis_size("ctx"), lax.axis_size("ch")

    def exchange(blocks):
        return lax.all_to_all(blocks, ("ctx", "ch"), split_axis=0, concat_axis=0)

    received = exchange(pack(inputs[0], grad_out[0], filters))
    dinputs, dfilters = unpack(exchange(unit(received, n_ctx, n_ch)))
    return dinputs[None], dfilters


def solution(mesh):
    placed = (P(None, "ch", "ctx"), P(None, "ch", "ctx"), P(None, "ctx"))
    return jax.shard_map(
        per_device,
        mesh=mesh,
        in_specs=placed,
        out_specs=(P(None, "ch", "ctx"), P(None, ("ctx", "ch"))),
        check_vma=False,
    )
```

```python
import functools
import math

import jax
import jax.numpy as jnp
import ml_dtypes
import numpy as np
from jax import lax
from jax.experimental import pallas as pl
from jax.experimental.pallas import tpu as pltpu
from jax.sharding import PartitionSpec as P

BF16 = jnp.bfloat16
F32 = jnp.float32
GROUP = 8
HALF = 128


def scaled(table):
    sizes, counts = np.unique(np.round(np.abs(table), 12), return_counts=True)

    def loss(factor):
        rounded = (sizes * factor).astype(ml_dtypes.bfloat16).astype(np.float64) / factor
        return np.sum(counts * (rounded - sizes) ** 2)

    factor = min(np.linspace(1.0, 2.0, 1025)[:-1], key=loss)
    return (table * factor), float(factor)


def make_tables(n_lead):
    points = n_lead * HALF
    shifted = np.arange(n_lead)[:, None] + 0.25
    angle = 2.0 * math.pi / n_lead * shifted * np.arange(n_lead)[None, :]
    lead, lead_factor = scaled(np.concatenate([np.cos(angle), -np.sin(angle)], 0))
    lead = np.kron(lead, np.eye(GROUP)).astype(ml_dtypes.bfloat16)
    turn = 2.0 * math.pi / points * shifted * np.arange(HALF)[None, :]
    turn = np.repeat(turn, GROUP, axis=0)
    twist = np.stack([np.cos(turn), -np.sin(turn)]).astype(np.float32)
    angle = 2.0 * math.pi / HALF * (np.arange(HALF)[:, None] * np.arange(HALF)[None, :] % HALF)
    cos, sin = np.cos(angle), np.sin(angle)
    trail, trail_factor = scaled(np.block([[cos, -sin], [sin, cos]]))
    undo = 1.0 / (points * (lead_factor * trail_factor) ** 3)
    return lead, np.ascontiguousarray(lead.T), trail.astype(ml_dtypes.bfloat16), twist, undo


def dot(left, right):
    return jnp.dot(left, right, preferred_element_type=F32)


def split(values):
    high = values.astype(BF16)
    return high, (values - high.astype(F32)).astype(BF16)


def unit_kernel(undo, recv_ref, lead_ref, back_ref, trail_ref, twist_ref, out_ref, filt_spec, cross):
    n_ctx, n_slab = recv_ref.shape[:2]
    rows = 2 * n_ctx * GROUP
    pair = 2 * GROUP

    def turn(real, imag):
        tw_re, tw_im = twist_ref[0], twist_ref[1]
        return jnp.concatenate([real * tw_re - imag * tw_im, real * tw_im + imag * tw_re], 1)

    def turn_back(second):
        imag, real = second[:, :HALF], second[:, HALF:]
        tw_re, tw_im = twist_ref[0], twist_ref[1]
        return jnp.concatenate([real * tw_re + imag * tw_im, imag * tw_re - real * tw_im], 0)

    def trail(values):
        return dot(values.astype(BF16), trail_ref[...])

    def trail_fine(values):
        high, low = split(values)
        return dot(high, trail_ref[...]) + dot(low, trail_ref[...])

    parts = [recv_ref[:, h, 2 * pair :].astype(F32).reshape(n_ctx, 1, GROUP, HALF) for h in (0, 1)]
    first = dot(lead_ref[...], jnp.concatenate(parts, 1).reshape(rows, HALF).astype(BF16))
    filt_spec[...] = trail_fine(turn(first[:rows], first[rows:])) * undo

    turned = []
    for slab in range(n_slab):
        both = [recv_ref[:, slab, k * pair : (k + 1) * pair].reshape(rows, HALF) for k in (0, 1)]
        first = dot(lead_ref[...], jnp.concatenate(both, 1))
        spec_in = trail(turn(first[:rows, :HALF], first[rows:, :HALF]))
        spec_grad = trail(turn(first[:rows, HALF:], first[rows:, HALF:]))
        in_re, in_im = spec_in[:, :HALF], spec_in[:, HALF:]
        grad_re, grad_im = spec_grad[:, :HALF], spec_grad[:, HALF:]
        cross_im = in_re * grad_im - in_im * grad_re
        cross_re = in_re * grad_re + in_im * grad_im
        if slab == 0:
            cross[:, :HALF] = cross_im
            cross[:, HALF:] = cross_re
        else:
            cross[:, :HALF] += cross_im
            cross[:, HALF:] += cross_re
        filt_re, filt_im = filt_spec[:, :HALF], filt_spec[:, HALF:]
        back_re = filt_re * grad_re + filt_im * grad_im
        back_im = filt_re * grad_im - filt_im * grad_re
        turned.append(turn_back(trail(jnp.concatenate([back_im, back_re], 1))).astype(BF16))
        if slab % 2 == 1:
            result = dot(back_ref[...], jnp.concatenate(turned[-2:], 1))
            for k in (0, 1):
                part = result[:, k * HALF : (k + 1) * HALF].astype(BF16)
                out_ref[:, slab - 1 + k, :pair] = part.reshape(n_ctx, pair, HALF)

    high, low = split(turn_back(trail_fine(cross[...])))
    result = dot(back_ref[...], jnp.concatenate([high, low], 1))
    result = (result[:, :HALF] + result[:, HALF:]) * undo
    result = result.reshape(n_ctx, 2, GROUP, HALF)
    for slab in range(n_slab):
        out_ref[:, slab, pair:] = result[:, slab // 2].astype(BF16)


def unit(received, n_ctx, n_slab):
    *tables, undo = make_tables(2 * n_ctx)
    spectra = pltpu.VMEM((2 * n_ctx * GROUP, 2 * HALF), F32)
    vmem = pl.BlockSpec(memory_space=pltpu.VMEM)
    out = pl.pallas_call(
        functools.partial(unit_kernel, undo),
        in_specs=[vmem] * 5,
        out_specs=vmem,
        out_shape=jax.ShapeDtypeStruct((n_ctx, n_slab, 3 * GROUP, HALF), BF16),
        scratch_shapes=[spectra, spectra],
        compiler_params=pltpu.CompilerParams(vmem_limit_bytes=40 * 2**20),
        name="unit",
    )(received.reshape(n_ctx, n_slab, 5 * GROUP, HALF), *[jnp.asarray(t) for t in tables])
    return out.reshape(n_ctx * n_slab, 3, GROUP, HALF)


def per_device(inputs, grad_out, filters):
    n_ctx, n_ch = lax.axis_size("ctx"), lax.axis_size("ch")
    parity = lax.axis_index("ch") & 1

    def tiles(values):
        return values.reshape(-1, GROUP, 2, HALF).transpose(0, 2, 1, 3)

    def exchange(blocks):
        return lax.all_to_all(blocks, ("ctx", "ch"), split_axis=0, concat_axis=0)

    half = lax.dynamic_slice_in_dim(tiles(filters), parity, 1, axis=1)
    packed = jnp.concatenate([tiles(inputs[0]), tiles(grad_out[0]), half], 1)
    returned = exchange(unit(exchange(packed), n_ctx, n_ch))
    dinputs = returned[:, :2].transpose(0, 2, 1, 3).reshape(inputs.shape)
    quarter = HALF // 2
    lane = lax.broadcasted_iota(jnp.int32, (quarter, HALF), 1)
    place = lax.broadcasted_iota(jnp.int32, (quarter, HALF), 0)
    pick = (lane == place + quarter * parity).astype(BF16)
    dfilters = lax.dot_general(
        pick, returned[:, 2].reshape(-1, HALF), (((1,), (1,)), ((), ())), preferred_element_type=F32
    )
    return dinputs, dfilters.T


def solution(mesh):
    placed = (P(None, "ch", "ctx"), P(None, "ch", "ctx"), P(None, "ctx"))
    return jax.shard_map(
        per_device,
        mesh=mesh,
        in_specs=placed,
        out_specs=(P(None, "ch", "ctx"), P(None, ("ctx", "ch"))),
        check_vma=False,
    )
```

```python
import functools
import math

import jax
import jax.numpy as jnp
import ml_dtypes
import numpy as np
from jax import lax
from jax.experimental import pallas as pl
from jax.experimental.pallas import tpu as pltpu
from jax.sharding import PartitionSpec as P

BF16 = jnp.bfloat16
F32 = jnp.float32
GROUP = 8
HALF = 128


def scaled(table):
    sizes, counts = np.unique(np.round(np.abs(table), 12), return_counts=True)

    def loss(factor):
        rounded = (sizes * factor).astype(ml_dtypes.bfloat16).astype(np.float64) / factor
        return np.sum(counts * (rounded - sizes) ** 2)

    factor = min(np.linspace(1.0, 2.0, 1025)[:-1], key=loss)
    return (table * factor), float(factor)


def make_tables(n_lead):
    points = n_lead * HALF
    shifted = np.arange(n_lead)[:, None] + 0.25
    angle = 2.0 * math.pi / n_lead * shifted * np.arange(n_lead)[None, :]
    lead, lead_factor = scaled(np.concatenate([np.cos(angle), -np.sin(angle)], 0))
    lead = np.kron(lead, np.eye(GROUP)).astype(ml_dtypes.bfloat16)
    turn = 2.0 * math.pi / points * shifted * np.arange(HALF)[None, :]
    turn = np.repeat(turn, GROUP, axis=0)
    twist = np.stack([np.cos(turn), -np.sin(turn)]).astype(np.float32)
    angle = 2.0 * math.pi / HALF * (np.arange(HALF)[:, None] * np.arange(HALF)[None, :] % HALF)
    cos, sin = np.cos(angle), np.sin(angle)
    trail, trail_factor = scaled(np.block([[cos, -sin], [sin, cos]]))
    undo = 1.0 / (points * (lead_factor * trail_factor) ** 3)
    return lead, np.ascontiguousarray(lead.T), trail.astype(ml_dtypes.bfloat16), twist, undo


def dot(left, right):
    return jnp.dot(left, right, preferred_element_type=F32)


def split(values):
    high = values.astype(BF16)
    return high, (values - high.astype(F32)).astype(BF16)


def unit_kernel(undo, recv_ref, lead_ref, back_ref, trail_ref, twist_ref, out_ref, filt_spec, cross):
    n_ctx, n_slab = recv_ref.shape[:2]
    rows = 2 * n_ctx * GROUP
    pair = 2 * GROUP

    def turn(real, imag):
        tw_re, tw_im = twist_ref[0], twist_ref[1]
        return jnp.concatenate([real * tw_re - imag * tw_im, real * tw_im + imag * tw_re], 1)

    def turn_back(second):
        imag, real = second[:, :HALF], second[:, HALF:]
        tw_re, tw_im = twist_ref[0], twist_ref[1]
        return jnp.concatenate([real * tw_re + imag * tw_im, imag * tw_re - real * tw_im], 0)

    def trail(values):
        return dot(values.astype(BF16), trail_ref[...])

    def trail_fine(values):
        high, low = split(values)
        return dot(high, trail_ref[...]) + dot(low, trail_ref[...])

    parts = [recv_ref[:, h, 2 * pair :].astype(F32).reshape(n_ctx, 1, GROUP, HALF) for h in (0, 1)]
    first = dot(lead_ref[...], jnp.concatenate(parts, 1).reshape(rows, HALF).astype(BF16))
    filt_spec[...] = trail_fine(turn(first[:rows], first[rows:])) * undo

    turned = []
    for slab in range(n_slab):
        both = [recv_ref[:, slab, k * pair : (k + 1) * pair].reshape(rows, HALF) for k in (0, 1)]
        first = dot(lead_ref[...], jnp.concatenate(both, 1))
        spec_in = trail(turn(first[:rows, :HALF], first[rows:, :HALF]))
        spec_grad = trail(turn(first[:rows, HALF:], first[rows:, HALF:]))
        in_re, in_im = spec_in[:, :HALF], spec_in[:, HALF:]
        grad_re, grad_im = spec_grad[:, :HALF], spec_grad[:, HALF:]
        cross_im = in_re * grad_im - in_im * grad_re
        cross_re = in_re * grad_re + in_im * grad_im
        if slab == 0:
            cross[:, :HALF] = cross_im
            cross[:, HALF:] = cross_re
        else:
            cross[:, :HALF] += cross_im
            cross[:, HALF:] += cross_re
        filt_re, filt_im = filt_spec[:, :HALF], filt_spec[:, HALF:]
        back_re = filt_re * grad_re + filt_im * grad_im
        back_im = filt_re * grad_im - filt_im * grad_re
        turned.append(turn_back(trail(jnp.concatenate([back_im, back_re], 1))).astype(BF16))
        if slab % 2 == 1:
            result = dot(back_ref[...], jnp.concatenate(turned[-2:], 1))
            for k in (0, 1):
                part = result[:, k * HALF : (k + 1) * HALF].astype(BF16)
                out_ref[:, slab - 1 + k, :pair] = part.reshape(n_ctx, pair, HALF)

    high, low = split(turn_back(trail_fine(cross[...])))
    result = dot(back_ref[...], jnp.concatenate([high, low], 1))
    result = (result[:, :HALF] + result[:, HALF:]) * undo
    result = result.reshape(n_ctx, 2, GROUP, HALF)
    for slab in range(n_slab):
        out_ref[:, slab, pair:] = result[:, slab // 2].astype(BF16)


def unit(received, n_ctx, n_slab):
    *tables, undo = make_tables(2 * n_ctx)
    spectra = pltpu.VMEM((2 * n_ctx * GROUP, 2 * HALF), F32)
    vmem = pl.BlockSpec(memory_space=pltpu.VMEM)
    out = pl.pallas_call(
        functools.partial(unit_kernel, undo),
        in_specs=[vmem] * 5,
        out_specs=vmem,
        out_shape=jax.ShapeDtypeStruct((n_ctx, n_slab, 3 * GROUP, HALF), BF16),
        scratch_shapes=[spectra, spectra],
        compiler_params=pltpu.CompilerParams(vmem_limit_bytes=40 * 2**20),
        name="unit",
    )(received.reshape(n_ctx, n_slab, 5 * GROUP, HALF), *[jnp.asarray(t) for t in tables])
    return out.reshape(n_ctx * n_slab, 3, GROUP, HALF)


def packed(inputs, grad_out, filters, even):
    def placed(values, low):
        tiles = values.reshape(-1, GROUP, 2, HALF).transpose(0, 2, 1, 3)
        none = (0, 0, 0)
        return lax.pad(tiles, jnp.zeros((), BF16), (none, (low, 3 - low, 0), none, none))

    tile = lax.broadcasted_iota(jnp.int32, (1, 5, 1, 1), 1)
    half = jnp.where(even, placed(filters, 4), placed(filters, 3))
    return jnp.where(tile < 2, placed(inputs, 0), jnp.where(tile < 4, placed(grad_out, 2), half))


def per_device(inputs, grad_out, filters):
    n_ctx, n_ch = lax.axis_size("ctx"), lax.axis_size("ch")
    even = lax.axis_index("ch") & 1 == 0

    def exchange(blocks):
        return lax.all_to_all(blocks, ("ctx", "ch"), split_axis=0, concat_axis=0)

    received = exchange(packed(inputs[0], grad_out[0], filters, even))
    returned = exchange(unit(received, n_ctx, n_ch))
    dinputs = returned[:, :2].transpose(0, 2, 1, 3).reshape(inputs.shape)
    eye = np.eye(HALF).astype(ml_dtypes.bfloat16)
    pick = jnp.where(even, jnp.asarray(eye[: HALF // 2]), jnp.asarray(eye[HALF // 2 :]))
    dfilters = lax.dot_general(
        pick, returned[:, 2].reshape(-1, HALF), (((1,), (1,)), ((), ())), preferred_element_type=F32
    )
    return dinputs, dfilters.T


def solution(mesh):
    placed = (P(None, "ch", "ctx"), P(None, "ch", "ctx"), P(None, "ctx"))
    return jax.shard_map(
        per_device,
        mesh=mesh,
        in_specs=placed,
        out_specs=(P(None, "ch", "ctx"), P(None, ("ctx", "ch"))),
        check_vma=False,
    )
```

```python
import functools
import math

import jax
import jax.numpy as jnp
import ml_dtypes
import numpy as np
from jax import lax
from jax.experimental import pallas as pl
from jax.experimental.pallas import tpu as pltpu
from jax.sharding import PartitionSpec as P

BF16 = jnp.bfloat16
F32 = jnp.float32
GROUP = 8
HALF = 128
RUN = 16


def scaled(table):
    sizes, counts = np.unique(np.round(np.abs(table), 12), return_counts=True)

    def loss(factor):
        rounded = (sizes * factor).astype(ml_dtypes.bfloat16).astype(np.float64) / factor
        return np.sum(counts * (rounded - sizes) ** 2)

    factor = min(np.linspace(1.0, 2.0, 1025)[:-1], key=loss)
    return (table * factor), float(factor)


def make_tables(n_lead):
    points = n_lead * HALF
    shifted = np.arange(n_lead)[:, None] + 0.25
    angle = 2.0 * math.pi / n_lead * shifted * np.arange(n_lead)[None, :]
    lead, lead_factor = scaled(np.concatenate([np.cos(angle), -np.sin(angle)], 0))
    lead = np.kron(lead, np.eye(GROUP)).astype(ml_dtypes.bfloat16)
    lead = lead.reshape(2, -1, RUN, lead.shape[1]).swapaxes(0, 1).reshape(lead.shape)
    turn = 2.0 * math.pi / points * shifted * np.arange(HALF)[None, :]
    turn = np.repeat(turn, GROUP, axis=0)
    twist = np.stack([np.cos(turn), -np.sin(turn)]).astype(np.float32)
    angle = 2.0 * math.pi / HALF * (np.arange(HALF)[:, None] * np.arange(HALF)[None, :] % HALF)
    cos, sin = np.cos(angle), np.sin(angle)
    trail, trail_factor = scaled(np.block([[cos, -sin], [sin, cos]]))
    undo = 1.0 / (points * (lead_factor * trail_factor) ** 3)
    return lead, np.ascontiguousarray(lead.T), trail.astype(ml_dtypes.bfloat16), twist, undo


def dot(left, right):
    return jnp.dot(left, right, preferred_element_type=F32)


def split(values):
    high = values.astype(BF16)
    return high, (values - high.astype(F32)).astype(BF16)


def unit_kernel(undo, recv_ref, lead_ref, back_ref, trail_ref, twist_ref, out_ref, filt_spec, cross):
    n_ctx, n_slab = recv_ref.shape[:2]
    rows = 2 * n_ctx * GROUP
    pair = 2 * GROUP

    def turn(first):
        real, imag = [first.reshape(-1, 2, RUN, HALF)[:, k].reshape(rows, HALF) for k in (0, 1)]
        tw_re, tw_im = twist_ref[0], twist_ref[1]
        return jnp.concatenate([real * tw_re - imag * tw_im, real * tw_im + imag * tw_re], 1)

    def turn_back(second):
        imag, real = second[:, :HALF], second[:, HALF:]
        tw_re, tw_im = twist_ref[0], twist_ref[1]
        parts = [real * tw_re + imag * tw_im, imag * tw_re - real * tw_im]
        return jnp.stack([part.reshape(-1, RUN, HALF) for part in parts], 1).reshape(2 * rows, HALF)

    def trail(values):
        return dot(values.astype(BF16), trail_ref[...])

    def trail_fine(values):
        high, low = split(values)
        return dot(high, trail_ref[...]) + dot(low, trail_ref[...])

    parts = [recv_ref[:, h, 2 * pair :].astype(F32).reshape(n_ctx, 1, GROUP, HALF) for h in (0, 1)]
    first = dot(lead_ref[...], jnp.concatenate(parts, 1).reshape(rows, HALF).astype(BF16))
    filt_spec[...] = trail_fine(turn(first)) * undo

    turned = []
    for slab in range(n_slab):
        both = [recv_ref[:, slab, k * pair : (k + 1) * pair].reshape(rows, HALF) for k in (0, 1)]
        first = dot(lead_ref[...], jnp.concatenate(both, 1))
        spec_in = trail(turn(first[:, :HALF]))
        spec_grad = trail(turn(first[:, HALF:]))
        in_re, in_im = spec_in[:, :HALF], spec_in[:, HALF:]
        grad_re, grad_im = spec_grad[:, :HALF], spec_grad[:, HALF:]
        cross_im = in_re * grad_im - in_im * grad_re
        cross_re = in_re * grad_re + in_im * grad_im
        if slab == 0:
            cross[:, :HALF] = cross_im
            cross[:, HALF:] = cross_re
        else:
            cross[:, :HALF] += cross_im
            cross[:, HALF:] += cross_re
        filt_re, filt_im = filt_spec[:, :HALF], filt_spec[:, HALF:]
        back_re = filt_re * grad_re + filt_im * grad_im
        back_im = filt_re * grad_im - filt_im * grad_re
        turned.append(turn_back(trail(jnp.concatenate([back_im, back_re], 1))).astype(BF16))
        if slab % 2 == 1:
            result = dot(back_ref[...], jnp.concatenate(turned[-2:], 1))
            for k in (0, 1):
                part = result[:, k * HALF : (k + 1) * HALF].astype(BF16)
                out_ref[:, slab - 1 + k, :pair] = part.reshape(n_ctx, pair, HALF)

    high, low = split(turn_back(trail_fine(cross[...])))
    result = dot(back_ref[...], jnp.concatenate([high, low], 1))
    result = (result[:, :HALF] + result[:, HALF:]) * undo
    result = result.reshape(n_ctx, 2, GROUP, HALF)
    for slab in range(n_slab):
        out_ref[:, slab, pair:] = result[:, slab // 2].astype(BF16)


def unit(received, n_ctx, n_slab):
    *tables, undo = make_tables(2 * n_ctx)
    spectra = pltpu.VMEM((2 * n_ctx * GROUP, 2 * HALF), F32)
    vmem = pl.BlockSpec(memory_space=pltpu.VMEM)
    out = pl.pallas_call(
        functools.partial(unit_kernel, undo),
        in_specs=[vmem] * 5,
        out_specs=vmem,
        out_shape=jax.ShapeDtypeStruct((n_ctx, n_slab, 3 * GROUP, HALF), BF16),
        scratch_shapes=[spectra, spectra],
        compiler_params=pltpu.CompilerParams(vmem_limit_bytes=40 * 2**20),
        name="unit",
    )(received.reshape(n_ctx, n_slab, 5 * GROUP, HALF), *[jnp.asarray(t) for t in tables])
    return out.reshape(n_ctx * n_slab, 3, GROUP, HALF)


def packed(inputs, grad_out, filters, even):
    def placed(values, low):
        tiles = values.reshape(-1, GROUP, 2, HALF).transpose(0, 2, 1, 3)
        none = (0, 0, 0)
        return lax.pad(tiles, jnp.zeros((), BF16), (none, (low, 3 - low, 0), none, none))

    tile = lax.broadcasted_iota(jnp.int32, (1, 5, 1, 1), 1)
    half = jnp.where(even, placed(filters, 4), placed(filters, 3))
    return jnp.where(tile < 2, placed(inputs, 0), jnp.where(tile < 4, placed(grad_out, 2), half))


def per_device(inputs, grad_out, filters):
    n_ctx, n_ch = lax.axis_size("ctx"), lax.axis_size("ch")
    even = lax.axis_index("ch") & 1 == 0

    def exchange(blocks):
        return lax.all_to_all(blocks, ("ctx", "ch"), split_axis=0, concat_axis=0)

    received = exchange(packed(inputs[0], grad_out[0], filters, even))
    returned = exchange(unit(received, n_ctx, n_ch))
    dinputs = returned[:, :2].transpose(0, 2, 1, 3).reshape(inputs.shape)
    eye = np.eye(HALF).astype(ml_dtypes.bfloat16)
    pick = jnp.where(even, jnp.asarray(eye[: HALF // 2]), jnp.asarray(eye[HALF // 2 :]))
    dfilters = lax.dot_general(
        pick, returned[:, 2].reshape(-1, HALF), (((1,), (1,)), ((), ())), preferred_element_type=F32
    )
    return dinputs, dfilters.T


def solution(mesh):
    placed = (P(None, "ch", "ctx"), P(None, "ch", "ctx"), P(None, "ctx"))
    return jax.shard_map(
        per_device,
        mesh=mesh,
        in_specs=placed,
        out_specs=(P(None, "ch", "ctx"), P(None, ("ctx", "ch"))),
        check_vma=False,
    )
```

```python
import functools
import math

import jax
import jax.numpy as jnp
import ml_dtypes
import numpy as np
from jax import lax
from jax.experimental import pallas as pl
from jax.experimental.pallas import tpu as pltpu
from jax.sharding import Mesh
from jax.sharding import PartitionSpec as P

BF16 = jnp.bfloat16
F32 = jnp.float32
GROUP = 8
HALF = 128
RUN = 16


def scaled(table):
    sizes, counts = np.unique(np.round(np.abs(table), 12), return_counts=True)

    def loss(factor):
        rounded = (sizes * factor).astype(ml_dtypes.bfloat16).astype(np.float64) / factor
        return np.sum(counts * (rounded - sizes) ** 2)

    factor = min(np.linspace(1.0, 2.0, 1025)[:-1], key=loss)
    return (table * factor), float(factor)


def make_tables(n_lead):
    points = n_lead * HALF
    shifted = np.arange(n_lead)[:, None] + 0.25
    angle = 2.0 * math.pi / n_lead * shifted * np.arange(n_lead)[None, :]
    lead, lead_factor = scaled(np.concatenate([np.cos(angle), -np.sin(angle)], 0))
    lead = np.kron(lead, np.eye(GROUP)).astype(ml_dtypes.bfloat16)
    lead = lead.reshape(2, -1, RUN, lead.shape[1]).swapaxes(0, 1).reshape(lead.shape)
    turn = 2.0 * math.pi / points * shifted * np.arange(HALF)[None, :]
    turn = np.repeat(turn, GROUP, axis=0)
    twist = np.stack([np.cos(turn), -np.sin(turn)]).astype(np.float32)
    angle = 2.0 * math.pi / HALF * (np.arange(HALF)[:, None] * np.arange(HALF)[None, :] % HALF)
    cos, sin = np.cos(angle), np.sin(angle)
    trail, trail_factor = scaled(np.block([[cos, -sin], [sin, cos]]))
    undo = 1.0 / (points * (lead_factor * trail_factor) ** 3)
    return lead, np.ascontiguousarray(lead.T), trail.astype(ml_dtypes.bfloat16), twist, undo


def dot(left, right):
    return jnp.dot(left, right, preferred_element_type=F32)


def split(values):
    high = values.astype(BF16)
    return high, (values - high.astype(F32)).astype(BF16)


def turned(first, twist_ref):
    real, imag = [first.reshape(-1, 2, RUN, HALF)[:, k].reshape(-1, HALF) for k in (0, 1)]
    tw_re, tw_im = twist_ref[0], twist_ref[1]
    return jnp.concatenate([real * tw_re - imag * tw_im, real * tw_im + imag * tw_re], 1)


def turned_back(second, twist_ref):
    imag, real = second[:, :HALF], second[:, HALF:]
    tw_re, tw_im = twist_ref[0], twist_ref[1]
    parts = [real * tw_re + imag * tw_im, imag * tw_re - real * tw_im]
    return jnp.stack([part.reshape(-1, RUN, HALF) for part in parts], 1).reshape(-1, HALF)


def sequences_kernel(undo, recv_ref, lead_ref, back_ref, trail_ref, twist_ref, spec_ref, part_ref, cross):
    n_ctx, n_slab = recv_ref.shape[:2]
    rows = 2 * n_ctx * GROUP
    pair = 2 * GROUP

    for slab in range(n_slab):
        for group in (0, 1):
            both = [
                recv_ref[:, slab, k * 2 * pair + group * pair : k * 2 * pair + (group + 1) * pair]
                for k in (0, 1)
            ]
            first = dot(lead_ref[...], jnp.concatenate([part.reshape(rows, HALF) for part in both], 1))
            spec_in = dot(turned(first[:, :HALF], twist_ref).astype(BF16), trail_ref[...])
            spec_grad = dot(turned(first[:, HALF:], twist_ref).astype(BF16), trail_ref[...])
            spec_ref[2 * slab + group] = spec_grad
            in_re, in_im = spec_in[:, :HALF], spec_in[:, HALF:]
            grad_re, grad_im = spec_grad[:, :HALF], spec_grad[:, HALF:]
            cross_im = in_re * grad_im - in_im * grad_re
            cross_re = in_re * grad_re + in_im * grad_im
            if slab == 0:
                cross[group, :, :HALF] = cross_im
                cross[group, :, HALF:] = cross_re
            else:
                cross[group, :, :HALF] += cross_im
                cross[group, :, HALF:] += cross_re

    parts = []
    for group in (0, 1):
        high, low = split(cross[group])
        second = dot(high, trail_ref[...]) + dot(low, trail_ref[...])
        parts.append(turned_back(second, twist_ref).astype(BF16))
    result = dot(back_ref[...], jnp.concatenate(parts, 1)) * undo
    for group in (0, 1):
        part = result[:, group * HALF : (group + 1) * HALF].astype(BF16)
        part_ref[:, group * pair : (group + 1) * pair] = part.reshape(n_ctx, pair, HALF)


def inverse_kernel(undo, own_ref, other_ref, spec_ref, lead_ref, back_ref, trail_ref, twist_ref, out_ref, filt_spec):
    n_ctx = own_ref.shape[0]
    n_slab = out_ref.shape[1]
    rows = 2 * n_ctx * GROUP
    pair = 2 * GROUP
    core = lax.axis_index("core")

    both = [ref[...].reshape(rows, HALF) for ref in (own_ref, other_ref)]
    first = dot(lead_ref[...], jnp.concatenate(both, 1))
    for k, group in ((0, core), (1, 1 - core)):
        high, low = split(turned(first[:, k * HALF : (k + 1) * HALF], twist_ref))
        filt_spec[group] = (dot(high, trail_ref[...]) + dot(low, trail_ref[...])) * undo

    for slab in range(n_slab):
        parts = []
        for group in (0, 1):
            grad_re, grad_im = spec_ref[2 * slab + group, :, :HALF], spec_ref[2 * slab + group, :, HALF:]
            filt_re, filt_im = filt_spec[group, :, :HALF], filt_spec[group, :, HALF:]
            back_re = filt_re * grad_re + filt_im * grad_im
            back_im = filt_re * grad_im - filt_im * grad_re
            product = jnp.concatenate([back_im, back_re], 1).astype(BF16)
            parts.append(turned_back(dot(product, trail_ref[...]), twist_ref).astype(BF16))
        result = dot(back_ref[...], jnp.concatenate(parts, 1))
        for group in (0, 1):
            part = result[:, group * HALF : (group + 1) * HALF].astype(BF16)
            out_ref[:, slab, group * pair : (group + 1) * pair] = part.reshape(n_ctx, pair, HALF)


def sum_kernel(mine_ref, other_ref, din_ref, out_ref):
    n_ctx = mine_ref.shape[0]
    pair = 2 * GROUP
    core = lax.axis_index("core")
    total = mine_ref[...].astype(F32) + other_ref[...].astype(F32)
    lane = lax.broadcasted_iota(jnp.int32, (n_ctx * GROUP, HALF), 1)
    out_ref[:, :, : 2 * pair] = din_ref[...]
    for h in (0, 1):
        first, second = [
            total[:, group * pair + h * GROUP : group * pair + (h + 1) * GROUP].reshape(n_ctx * GROUP, HALF)
            for group in (0, 1)
        ]
        first = jnp.where(core == 0, first, pltpu.roll(first, HALF // 2, 1))
        second = jnp.where(core == 0, pltpu.roll(second, HALF // 2, 1), second)
        both = jnp.where(lane < HALF // 2, first, second)
        out_ref[:, h, 2 * pair :] = both.reshape(n_ctx, GROUP, HALF).astype(BF16)


def packed(inputs, grad_out, filters, core, y_hi):
    def tiles(values):
        split_up = values.reshape(-1, 2, GROUP, 2, HALF).transpose(0, 1, 3, 2, 4)
        return split_up.reshape(-1, 4, GROUP, HALF)

    none = (0, 0, 0)

    def placed(values, low, high):
        return lax.pad(tiles(values), jnp.zeros((), BF16), (none, (low, high, 0), none, none))

    tile = lax.broadcasted_iota(jnp.int32, (1, 9, 1, 1), 1)
    last = placed(filters, 8, 0)
    last = lax.dynamic_slice_in_dim(last, 2 * core + y_hi, 9, axis=1)
    return jnp.where(tile < 4, placed(inputs, 0, 5), jnp.where(tile < 8, placed(grad_out, 4, 1), last))


def per_device(inputs, grad_out, filters):
    n_ctx, n_slab = lax.axis_size("ctx"), lax.axis_size("y_hi")
    rows = 2 * n_ctx * GROUP
    lead, back, trail, twist, undo = make_tables(2 * n_ctx)
    lead, back, trail, twist = [jnp.asarray(table) for table in (lead, back, trail, twist)]
    vmem = pl.BlockSpec(memory_space=pltpu.VMEM)
    spectra = pltpu.VMEM((2, rows, 2 * HALF), F32)

    def kernel(body, name, operands, out_shape, scratch, flops):
        several = isinstance(out_shape, tuple)
        return pl.pallas_call(
            body,
            in_specs=[vmem] * len(operands),
            out_specs=tuple(vmem for _ in out_shape) if several else vmem,
            out_shape=out_shape,
            scratch_shapes=scratch,
            compiler_params=pltpu.CompilerParams(vmem_limit_bytes=40 * 2**20),
            cost_estimate=pl.CostEstimate(flops=flops, bytes_accessed=2**21, transcendentals=0),
            name=name,
        )(*operands)

    def exchange(blocks):
        return lax.all_to_all(blocks, ("ctx", "y_hi"), split_axis=0, concat_axis=0)

    def swapped(values):
        return lax.ppermute(values, "core", ((0, 1), (1, 0)))

    def shape(*sizes, dtype=BF16):
        return jax.ShapeDtypeStruct(sizes, dtype)

    received = exchange(packed(inputs[0], grad_out[0], filters, lax.axis_index("core"), lax.axis_index("y_hi")))
    own = received[:, 8].reshape(n_ctx, 2 * GROUP, HALF)
    other = swapped(own)
    received = received.reshape(n_ctx, n_slab, 9 * GROUP, HALF)
    spec_grad, mine = kernel(
        functools.partial(sequences_kernel, undo),
        "sequences",
        (received, lead, back, trail, twist),
        (shape(2 * n_slab, rows, 2 * HALF, dtype=F32), shape(n_ctx, 4 * GROUP, HALF)),
        [spectra],
        4 * 10**9,
    )
    theirs = swapped(mine)
    din = kernel(
        functools.partial(inverse_kernel, undo),
        "inverse",
        (own, other, spec_grad, lead, back, trail, twist),
        shape(n_ctx, n_slab, 4 * GROUP, HALF),
        [spectra],
        3 * 10**9,
    )
    returned = kernel(sum_kernel, "sum", (mine, theirs, din), shape(n_ctx, n_slab, 5 * GROUP, HALF), [], 10**6)
    returned = exchange(returned.reshape(n_ctx * n_slab, 5, GROUP, HALF))
    dinputs = returned[:, :4].reshape(-1, 2, 2, GROUP, HALF).transpose(0, 1, 3, 2, 4).reshape(inputs.shape)
    side = jnp.asarray(np.repeat(np.eye(2), HALF // 2, axis=1).reshape(1, 2, 1, HALF) > 0)
    both = jnp.where(side, returned[:, 4][:, None], jnp.zeros((), BF16)).reshape(-1, HALF)
    eye = np.eye(HALF // 2)
    pick = jnp.asarray(np.concatenate([eye, eye], 1).astype(ml_dtypes.bfloat16))
    dfilters = lax.dot_general(pick, both, (((1,), (1,)), ((), ())), preferred_element_type=F32)
    return dinputs, dfilters.T


def solution(mesh):
    n_ctx, n_ch = mesh.devices.shape
    fine = Mesh(mesh.devices.reshape(n_ctx, n_ch // 2, 2), ("ctx", "y_hi", "core"))
    channels = ("y_hi", "core")
    placed = (P(None, channels, "ctx"), P(None, channels, "ctx"), P(None, "ctx"))
    return jax.shard_map(
        per_device,
        mesh=fine,
        in_specs=placed,
        out_specs=(P(None, channels, "ctx"), P(None, ("ctx",) + channels)),
        check_vma=False,
    )
```

```python
import functools
import math

import jax
import jax.numpy as jnp
import ml_dtypes
import numpy as np
from jax import lax
from jax.experimental import pallas as pl
from jax.experimental.pallas import tpu as pltpu
from jax.sharding import Mesh
from jax.sharding import PartitionSpec as P

BF16 = jnp.bfloat16
F32 = jnp.float32
GROUP = 8
HALF = 128
RUN = 16


def scaled(table):
    sizes, counts = np.unique(np.round(np.abs(table), 12), return_counts=True)

    def loss(factor):
        rounded = (sizes * factor).astype(ml_dtypes.bfloat16).astype(np.float64) / factor
        return np.sum(counts * (rounded - sizes) ** 2)

    factor = min(np.linspace(1.0, 2.0, 1025)[:-1], key=loss)
    return (table * factor), float(factor)


def make_tables(n_lead):
    points = n_lead * HALF
    shifted = np.arange(n_lead)[:, None] + 0.25
    angle = 2.0 * math.pi / n_lead * shifted * np.arange(n_lead)[None, :]
    lead, lead_factor = scaled(np.concatenate([np.cos(angle), -np.sin(angle)], 0))
    lead = np.kron(lead, np.eye(GROUP)).astype(ml_dtypes.bfloat16)
    lead = lead.reshape(2, -1, RUN, lead.shape[1]).swapaxes(0, 1).reshape(lead.shape)
    turn = 2.0 * math.pi / points * shifted * np.arange(HALF)[None, :]
    turn = np.repeat(turn, GROUP, axis=0)
    twist = np.stack([np.cos(turn), -np.sin(turn)]).astype(np.float32)
    angle = 2.0 * math.pi / HALF * (np.arange(HALF)[:, None] * np.arange(HALF)[None, :] % HALF)
    cos, sin = np.cos(angle), np.sin(angle)
    trail, trail_factor = scaled(np.block([[cos, -sin], [sin, cos]]))
    undo = 1.0 / (points * (lead_factor * trail_factor) ** 3)
    return lead, np.ascontiguousarray(lead.T), trail.astype(ml_dtypes.bfloat16), twist, undo


def dot(left, right):
    return jnp.dot(left, right, preferred_element_type=F32)


def split(values):
    high = values.astype(BF16)
    return high, (values - high.astype(F32)).astype(BF16)


def turned(first, twist_ref):
    real, imag = [first.reshape(-1, 2, RUN, HALF)[:, k].reshape(-1, HALF) for k in (0, 1)]
    tw_re, tw_im = twist_ref[0], twist_ref[1]
    return jnp.concatenate([real * tw_re - imag * tw_im, real * tw_im + imag * tw_re], 1)


def turned_back(second, twist_ref):
    imag, real = second[:, :HALF], second[:, HALF:]
    tw_re, tw_im = twist_ref[0], twist_ref[1]
    parts = [real * tw_re + imag * tw_im, imag * tw_re - real * tw_im]
    return jnp.stack([part.reshape(-1, RUN, HALF) for part in parts], 1).reshape(-1, HALF)


def sequences_kernel(undo, recv_ref, lead_ref, back_ref, trail_ref, twist_ref, spec_ref, part_ref, cross):
    n_ctx, n_slab = recv_ref.shape[:2]
    rows = 2 * n_ctx * GROUP
    pair = 2 * GROUP

    parts = []
    for group in (0, 1):
        for slab in range(n_slab):
            both = [
                recv_ref[:, slab, k * 2 * pair + group * pair : k * 2 * pair + (group + 1) * pair]
                for k in (0, 1)
            ]
            first = dot(lead_ref[...], jnp.concatenate([part.reshape(rows, HALF) for part in both], 1))
            spec_in = dot(turned(first[:, :HALF], twist_ref).astype(BF16), trail_ref[...])
            spec_grad = dot(turned(first[:, HALF:], twist_ref).astype(BF16), trail_ref[...])
            spec_ref[2 * slab + group] = spec_grad
            in_re, in_im = spec_in[:, :HALF], spec_in[:, HALF:]
            grad_re, grad_im = spec_grad[:, :HALF], spec_grad[:, HALF:]
            cross_im = in_re * grad_im - in_im * grad_re
            cross_re = in_re * grad_re + in_im * grad_im
            if slab == 0:
                cross[group, :, :HALF] = cross_im
                cross[group, :, HALF:] = cross_re
            else:
                cross[group, :, :HALF] += cross_im
                cross[group, :, HALF:] += cross_re

        high, low = split(cross[group])
        second = dot(high, trail_ref[...]) + dot(low, trail_ref[...])
        parts.append(turned_back(second, twist_ref).astype(BF16))
    result = dot(back_ref[...], jnp.concatenate(parts, 1)) * undo
    for group in (0, 1):
        part = result[:, group * HALF : (group + 1) * HALF].astype(BF16)
        part_ref[:, group * pair : (group + 1) * pair] = part.reshape(n_ctx, pair, HALF)


def inverse_kernel(undo, own_ref, other_ref, spec_ref, lead_ref, back_ref, trail_ref, twist_ref, out_ref, filt_spec):
    n_ctx = own_ref.shape[0]
    n_slab = out_ref.shape[1]
    rows = 2 * n_ctx * GROUP
    pair = 2 * GROUP
    core = lax.axis_index("core")

    both = [ref[...].reshape(rows, HALF) for ref in (own_ref, other_ref)]
    first = dot(lead_ref[...], jnp.concatenate(both, 1))
    for k, group in ((0, core), (1, 1 - core)):
        high, low = split(turned(first[:, k * HALF : (k + 1) * HALF], twist_ref))
        filt_spec[group] = (dot(high, trail_ref[...]) + dot(low, trail_ref[...])) * undo

    for slab in range(n_slab):
        parts = []
        for group in (0, 1):
            grad_re, grad_im = spec_ref[2 * slab + group, :, :HALF], spec_ref[2 * slab + group, :, HALF:]
            filt_re, filt_im = filt_spec[group, :, :HALF], filt_spec[group, :, HALF:]
            back_re = filt_re * grad_re + filt_im * grad_im
            back_im = filt_re * grad_im - filt_im * grad_re
            product = jnp.concatenate([back_im, back_re], 1).astype(BF16)
            parts.append(turned_back(dot(product, trail_ref[...]), twist_ref).astype(BF16))
        result = dot(back_ref[...], jnp.concatenate(parts, 1))
        for group in (0, 1):
            part = result[:, group * HALF : (group + 1) * HALF].astype(BF16)
            out_ref[:, slab, group * pair : (group + 1) * pair] = part.reshape(n_ctx, pair, HALF)


def sum_kernel(mine_ref, other_ref, din_ref, out_ref):
    n_ctx = mine_ref.shape[0]
    pair = 2 * GROUP
    core = lax.axis_index("core")
    total = mine_ref[...].astype(F32) + other_ref[...].astype(F32)
    lane = lax.broadcasted_iota(jnp.int32, (n_ctx * GROUP, HALF), 1)
    out_ref[:, :, : 2 * pair] = din_ref[...]
    for h in (0, 1):
        first, second = [
            total[:, group * pair + h * GROUP : group * pair + (h + 1) * GROUP].reshape(n_ctx * GROUP, HALF)
            for group in (0, 1)
        ]
        first = jnp.where(core == 0, first, pltpu.roll(first, HALF // 2, 1))
        second = jnp.where(core == 0, pltpu.roll(second, HALF // 2, 1), second)
        both = jnp.where(lane < HALF // 2, first, second)
        out_ref[:, h, 2 * pair :] = both.reshape(n_ctx, GROUP, HALF).astype(BF16)


def packed(inputs, grad_out, filters, core, y_hi):
    def tiles(values):
        split_up = values.reshape(-1, 2, GROUP, 2, HALF).transpose(0, 1, 3, 2, 4)
        return split_up.reshape(-1, 4, GROUP, HALF)

    none = (0, 0, 0)

    def placed(values, low, high):
        return lax.pad(tiles(values), jnp.zeros((), BF16), (none, (low, high, 0), none, none))

    tile = lax.broadcasted_iota(jnp.int32, (1, 9, 1, 1), 1)
    last = placed(filters, 8, 0)
    last = lax.dynamic_slice_in_dim(last, 2 * core + y_hi, 9, axis=1)
    return jnp.where(tile < 4, placed(inputs, 0, 5), jnp.where(tile < 8, placed(grad_out, 4, 1), last))


def per_device(inputs, grad_out, filters):
    n_ctx, n_slab = lax.axis_size("ctx"), lax.axis_size("y_hi")
    rows = 2 * n_ctx * GROUP
    lead, back, trail, twist, undo = make_tables(2 * n_ctx)
    lead, back, trail, twist = [jnp.asarray(table) for table in (lead, back, trail, twist)]
    vmem = pl.BlockSpec(memory_space=pltpu.VMEM)
    spectra = pltpu.VMEM((2, rows, 2 * HALF), F32)

    def kernel(body, name, operands, out_shape, scratch, flops):
        several = isinstance(out_shape, tuple)
        return pl.pallas_call(
            body,
            in_specs=[vmem] * len(operands),
            out_specs=tuple(vmem for _ in out_shape) if several else vmem,
            out_shape=out_shape,
            scratch_shapes=scratch,
            compiler_params=pltpu.CompilerParams(vmem_limit_bytes=40 * 2**20),
            cost_estimate=pl.CostEstimate(flops=flops, bytes_accessed=2**21, transcendentals=0),
            name=name,
        )(*operands)

    def exchange(blocks):
        return lax.all_to_all(blocks, ("ctx", "y_hi"), split_axis=0, concat_axis=0)

    def swapped(values):
        return lax.ppermute(values, "core", ((0, 1), (1, 0)))

    def shape(*sizes, dtype=BF16):
        return jax.ShapeDtypeStruct(sizes, dtype)

    received = exchange(packed(inputs[0], grad_out[0], filters, lax.axis_index("core"), lax.axis_index("y_hi")))
    own = received[:, 8].reshape(n_ctx, 2 * GROUP, HALF)
    other = swapped(own)
    received = received.reshape(n_ctx, n_slab, 9 * GROUP, HALF)
    spec_grad, mine = kernel(
        functools.partial(sequences_kernel, undo),
        "sequences",
        (received, lead, back, trail, twist),
        (shape(2 * n_slab, rows, 2 * HALF, dtype=F32), shape(n_ctx, 4 * GROUP, HALF)),
        [spectra],
        4 * 10**9,
    )
    theirs = swapped(mine)
    din = kernel(
        functools.partial(inverse_kernel, undo),
        "inverse",
        (own, other, spec_grad, lead, back, trail, twist),
        shape(n_ctx, n_slab, 4 * GROUP, HALF),
        [spectra],
        3 * 10**9,
    )
    returned = kernel(sum_kernel, "sum", (mine, theirs, din), shape(n_ctx, n_slab, 5 * GROUP, HALF), [], 10**6)
    returned = exchange(returned.reshape(n_ctx * n_slab, 5, GROUP, HALF))
    dinputs = returned[:, :4].reshape(-1, 2, 2, GROUP, HALF).transpose(0, 1, 3, 2, 4).reshape(inputs.shape)
    side = jnp.asarray(np.repeat(np.eye(2), HALF // 2, axis=1).reshape(1, 2, 1, HALF) > 0)
    both = jnp.where(side, returned[:, 4][:, None], jnp.zeros((), BF16)).reshape(-1, HALF)
    eye = np.eye(HALF // 2)
    pick = jnp.asarray(np.concatenate([eye, eye], 1).astype(ml_dtypes.bfloat16))
    dfilters = lax.dot_general(pick, both, (((1,), (1,)), ((), ())), preferred_element_type=F32)
    return dinputs, dfilters.T


def solution(mesh):
    n_ctx, n_ch = mesh.devices.shape
    fine = Mesh(mesh.devices.reshape(n_ctx, n_ch // 2, 2), ("ctx", "y_hi", "core"))
    channels = ("y_hi", "core")
    placed = (P(None, channels, "ctx"), P(None, channels, "ctx"), P(None, "ctx"))
    return jax.shard_map(
        per_device,
        mesh=fine,
        in_specs=placed,
        out_specs=(P(None, channels, "ctx"), P(None, ("ctx",) + channels)),
        check_vma=False,
    )
```

```python
import functools
import math

import jax
import jax.numpy as jnp
import ml_dtypes
import numpy as np
from jax import lax
from jax.experimental import pallas as pl
from jax.experimental.pallas import tpu as pltpu
from jax.sharding import Mesh
from jax.sharding import PartitionSpec as P

BF16 = jnp.bfloat16
F32 = jnp.float32
GROUP = 8
HALF = 128
RUN = 16


def scaled(table):
    sizes, counts = np.unique(np.round(np.abs(table), 12), return_counts=True)

    def loss(factor):
        rounded = (sizes * factor).astype(ml_dtypes.bfloat16).astype(np.float64) / factor
        return np.sum(counts * (rounded - sizes) ** 2)

    factor = min(np.linspace(1.0, 2.0, 1025)[:-1], key=loss)
    return (table * factor), float(factor)


def make_tables(n_lead):
    points = n_lead * HALF
    shifted = np.arange(n_lead)[:, None] + 0.25
    angle = 2.0 * math.pi / n_lead * shifted * np.arange(n_lead)[None, :]
    lead, lead_factor = scaled(np.concatenate([np.cos(angle), -np.sin(angle)], 0))
    lead = np.kron(lead, np.eye(GROUP)).astype(ml_dtypes.bfloat16)
    lead = lead.reshape(2, -1, RUN, lead.shape[1]).swapaxes(0, 1).reshape(lead.shape)
    turn = 2.0 * math.pi / points * shifted * np.arange(HALF)[None, :]
    turn = np.repeat(turn, GROUP, axis=0)
    twist = np.stack([np.cos(turn), -np.sin(turn)]).astype(np.float32)
    angle = 2.0 * math.pi / HALF * (np.arange(HALF)[:, None] * np.arange(HALF)[None, :] % HALF)
    cos, sin = np.cos(angle), np.sin(angle)
    trail, trail_factor = scaled(np.block([[cos, -sin], [sin, cos]]))
    undo = 1.0 / (points * (lead_factor * trail_factor) ** 3)
    return lead, np.ascontiguousarray(lead.T), trail.astype(ml_dtypes.bfloat16), twist, undo


def dot(left, right):
    return jnp.dot(left, right, preferred_element_type=F32)


def split(values):
    high = values.astype(BF16)
    return high, (values - high.astype(F32)).astype(BF16)


def turned(first, twist_ref):
    real, imag = [first.reshape(-1, 2, RUN, HALF)[:, k].reshape(-1, HALF) for k in (0, 1)]
    tw_re, tw_im = twist_ref[0], twist_ref[1]
    return jnp.concatenate([real * tw_re - imag * tw_im, real * tw_im + imag * tw_re], 1)


def turned_back(second, twist_ref):
    imag, real = second[:, :HALF], second[:, HALF:]
    tw_re, tw_im = twist_ref[0], twist_ref[1]
    parts = [real * tw_re + imag * tw_im, imag * tw_re - real * tw_im]
    return jnp.stack([part.reshape(-1, RUN, HALF) for part in parts], 1).reshape(-1, HALF)


def sequences_kernel(undo, recv_ref, lead_ref, back_ref, trail_ref, twist_ref, spec_ref, part_ref, cross):
    n_ctx, n_slab = recv_ref.shape[:2]
    rows = 2 * n_ctx * GROUP
    pair = 2 * GROUP

    parts = []
    for group in (0, 1):
        for slab in range(n_slab):
            both = [
                recv_ref[:, slab, k * 2 * pair + group * pair : k * 2 * pair + (group + 1) * pair]
                for k in (0, 1)
            ]
            first = dot(lead_ref[...], jnp.concatenate([part.reshape(rows, HALF) for part in both], 1))
            spec_in = dot(turned(first[:, :HALF], twist_ref).astype(BF16), trail_ref[...])
            spec_grad = dot(turned(first[:, HALF:], twist_ref).astype(BF16), trail_ref[...])
            spec_ref[2 * slab + group] = spec_grad
            in_re, in_im = spec_in[:, :HALF], spec_in[:, HALF:]
            grad_re, grad_im = spec_grad[:, :HALF], spec_grad[:, HALF:]
            cross_im = in_re * grad_im - in_im * grad_re
            cross_re = in_re * grad_re + in_im * grad_im
            if slab == 0:
                cross[group, :, :HALF] = cross_im
                cross[group, :, HALF:] = cross_re
            else:
                cross[group, :, :HALF] += cross_im
                cross[group, :, HALF:] += cross_re

        high, low = split(cross[group])
        second = dot(high, trail_ref[...]) + dot(low, trail_ref[...])
        parts.append(turned_back(second, twist_ref).astype(BF16))
    result = dot(back_ref[...], jnp.concatenate(parts, 1)) * undo
    for group in (0, 1):
        part = result[:, group * HALF : (group + 1) * HALF].astype(BF16)
        part_ref[:, group * pair : (group + 1) * pair] = part.reshape(n_ctx, pair, HALF)


def inverse_kernel(undo, own_ref, other_ref, spec_ref, lead_ref, back_ref, trail_ref, twist_ref, out_ref):
    n_ctx = own_ref.shape[0]
    n_slab = out_ref.shape[1]
    rows = 2 * n_ctx * GROUP
    pair = 2 * GROUP
    core = lax.axis_index("core")

    both = [ref[...].reshape(rows, HALF) for ref in (own_ref, other_ref)]
    first = dot(lead_ref[...], jnp.concatenate(both, 1))
    parts = [[] for _ in range(n_slab)]
    for k, group in ((0, core), (1, 1 - core)):
        high, low = split(turned(first[:, k * HALF : (k + 1) * HALF], twist_ref))
        filt = (dot(high, trail_ref[...]) + dot(low, trail_ref[...])) * undo
        filt_re, filt_im = filt[:, :HALF], filt[:, HALF:]
        for slab in range(n_slab):
            grad_re, grad_im = spec_ref[2 * slab + group, :, :HALF], spec_ref[2 * slab + group, :, HALF:]
            back_re = filt_re * grad_re + filt_im * grad_im
            back_im = filt_re * grad_im - filt_im * grad_re
            product = jnp.concatenate([back_im, back_re], 1).astype(BF16)
            parts[slab].append(turned_back(dot(product, trail_ref[...]), twist_ref).astype(BF16))
    for slab in range(n_slab):
        result = dot(back_ref[...], jnp.concatenate(parts[slab], 1))
        for k, group in ((0, core), (1, 1 - core)):
            part = result[:, k * HALF : (k + 1) * HALF].astype(BF16)
            out_ref[:, slab, pl.ds(pl.multiple_of(group * pair, pair), pair)] = part.reshape(n_ctx, pair, HALF)


def sum_kernel(mine_ref, other_ref, din_ref, out_ref):
    n_ctx = mine_ref.shape[0]
    pair = 2 * GROUP
    core = lax.axis_index("core")
    total = mine_ref[...].astype(F32) + other_ref[...].astype(F32)
    lane = lax.broadcasted_iota(jnp.int32, (n_ctx * GROUP, HALF), 1)
    out_ref[:, :, : 2 * pair] = din_ref[...]
    for h in (0, 1):
        first, second = [
            total[:, group * pair + h * GROUP : group * pair + (h + 1) * GROUP].reshape(n_ctx * GROUP, HALF)
            for group in (0, 1)
        ]
        first = jnp.where(core == 0, first, pltpu.roll(first, HALF // 2, 1))
        second = jnp.where(core == 0, pltpu.roll(second, HALF // 2, 1), second)
        both = jnp.where(lane < HALF // 2, first, second)
        out_ref[:, h, 2 * pair :] = both.reshape(n_ctx, GROUP, HALF).astype(BF16)


def packed(inputs, grad_out, filters, core, y_hi):
    def tiles(values):
        split_up = values.reshape(-1, 2, GROUP, 2, HALF).transpose(0, 1, 3, 2, 4)
        return split_up.reshape(-1, 4, GROUP, HALF)

    none = (0, 0, 0)

    def placed(values, low, high):
        return lax.pad(tiles(values), jnp.zeros((), BF16), (none, (low, high, 0), none, none))

    tile = lax.broadcasted_iota(jnp.int32, (1, 9, 1, 1), 1)
    last = placed(filters, 8, 0)
    last = lax.dynamic_slice_in_dim(last, 2 * core + y_hi, 9, axis=1)
    return jnp.where(tile < 4, placed(inputs, 0, 5), jnp.where(tile < 8, placed(grad_out, 4, 1), last))


def per_device(inputs, grad_out, filters):
    n_ctx, n_slab = lax.axis_size("ctx"), lax.axis_size("y_hi")
    rows = 2 * n_ctx * GROUP
    lead, back, trail, twist, undo = make_tables(2 * n_ctx)
    lead, back, trail, twist = [jnp.asarray(table) for table in (lead, back, trail, twist)]
    vmem = pl.BlockSpec(memory_space=pltpu.VMEM)
    spectra = pltpu.VMEM((2, rows, 2 * HALF), F32)

    def kernel(body, name, operands, out_shape, scratch, flops):
        several = isinstance(out_shape, tuple)
        return pl.pallas_call(
            body,
            in_specs=[vmem] * len(operands),
            out_specs=tuple(vmem for _ in out_shape) if several else vmem,
            out_shape=out_shape,
            scratch_shapes=scratch,
            compiler_params=pltpu.CompilerParams(vmem_limit_bytes=40 * 2**20),
            cost_estimate=pl.CostEstimate(flops=flops, bytes_accessed=2**21, transcendentals=0),
            name=name,
        )(*operands)

    def exchange(blocks):
        return lax.all_to_all(blocks, ("ctx", "y_hi"), split_axis=0, concat_axis=0)

    def swapped(values):
        return lax.ppermute(values, "core", ((0, 1), (1, 0)))

    def shape(*sizes, dtype=BF16):
        return jax.ShapeDtypeStruct(sizes, dtype)

    received = exchange(packed(inputs[0], grad_out[0], filters, lax.axis_index("core"), lax.axis_index("y_hi")))
    own = received[:, 8].reshape(n_ctx, 2 * GROUP, HALF)
    other = swapped(own)
    received = received.reshape(n_ctx, n_slab, 9 * GROUP, HALF)
    spec_grad, mine = kernel(
        functools.partial(sequences_kernel, undo),
        "sequences",
        (received, lead, back, trail, twist),
        (shape(2 * n_slab, rows, 2 * HALF, dtype=F32), shape(n_ctx, 4 * GROUP, HALF)),
        [spectra],
        4 * 10**9,
    )
    theirs = swapped(mine)
    din = kernel(
        functools.partial(inverse_kernel, undo),
        "inverse",
        (own, other, spec_grad, lead, back, trail, twist),
        shape(n_ctx, n_slab, 4 * GROUP, HALF),
        [],
        3 * 10**9,
    )
    returned = kernel(sum_kernel, "sum", (mine, theirs, din), shape(n_ctx, n_slab, 5 * GROUP, HALF), [], 10**6)
    returned = exchange(returned.reshape(n_ctx * n_slab, 5, GROUP, HALF))
    dinputs = returned[:, :4].reshape(-1, 2, 2, GROUP, HALF).transpose(0, 1, 3, 2, 4).reshape(inputs.shape)
    side = jnp.asarray(np.repeat(np.eye(2), HALF // 2, axis=1).reshape(1, 2, 1, HALF) > 0)
    both = jnp.where(side, returned[:, 4][:, None], jnp.zeros((), BF16)).reshape(-1, HALF)
    eye = np.eye(HALF // 2)
    pick = jnp.asarray(np.concatenate([eye, eye], 1).astype(ml_dtypes.bfloat16))
    dfilters = lax.dot_general(pick, both, (((1,), (1,)), ((), ())), preferred_element_type=F32)
    return dinputs, dfilters.T


def solution(mesh):
    n_ctx, n_ch = mesh.devices.shape
    fine = Mesh(mesh.devices.reshape(n_ctx, n_ch // 2, 2), ("ctx", "y_hi", "core"))
    channels = ("y_hi", "core")
    placed = (P(None, channels, "ctx"), P(None, channels, "ctx"), P(None, "ctx"))
    return jax.shard_map(
        per_device,
        mesh=fine,
        in_specs=placed,
        out_specs=(P(None, channels, "ctx"), P(None, ("ctx",) + channels)),
        check_vma=False,
    )
```

```python
import functools
import math

import jax
import jax.numpy as jnp
import ml_dtypes
import numpy as np
from jax import lax
from jax.experimental import pallas as pl
from jax.experimental.pallas import tpu as pltpu
from jax.sharding import Mesh
from jax.sharding import PartitionSpec as P

BF16 = jnp.bfloat16
F32 = jnp.float32
GROUP = 8
HALF = 128
RUN = 16


def scaled(table):
    sizes, counts = np.unique(np.round(np.abs(table), 12), return_counts=True)

    def loss(factor):
        rounded = (sizes * factor).astype(ml_dtypes.bfloat16).astype(np.float64) / factor
        return np.sum(counts * (rounded - sizes) ** 2)

    factor = min(np.linspace(1.0, 2.0, 1025)[:-1], key=loss)
    return (table * factor), float(factor)


def make_tables(n_lead):
    points = n_lead * HALF
    shifted = np.arange(n_lead)[:, None] + 0.25
    angle = 2.0 * math.pi / n_lead * shifted * np.arange(n_lead)[None, :]
    lead, lead_factor = scaled(np.concatenate([np.cos(angle), -np.sin(angle)], 0))
    lead = np.kron(lead, np.eye(GROUP)).astype(ml_dtypes.bfloat16)
    lead = lead.reshape(2, -1, RUN, lead.shape[1]).swapaxes(0, 1).reshape(lead.shape)
    turn = 2.0 * math.pi / points * shifted * np.arange(HALF)[None, :]
    turn = np.repeat(turn, GROUP, axis=0)
    twist = np.stack([np.cos(turn), -np.sin(turn)]).astype(np.float32)
    angle = 2.0 * math.pi / HALF * (np.arange(HALF)[:, None] * np.arange(HALF)[None, :] % HALF)
    cos, sin = np.cos(angle), np.sin(angle)
    trail, trail_factor = scaled(np.block([[cos, -sin], [sin, cos]]))
    undo = 1.0 / (points * (lead_factor * trail_factor) ** 3)
    return lead, np.ascontiguousarray(lead.T), trail.astype(ml_dtypes.bfloat16), twist, undo


def dot(left, right):
    return jnp.dot(left, right, preferred_element_type=F32)


def split(values):
    high = values.astype(BF16)
    return high, (values - high.astype(F32)).astype(BF16)


def turned(first, twist_ref):
    real, imag = [first.reshape(-1, 2, RUN, HALF)[:, k].reshape(-1, HALF) for k in (0, 1)]
    tw_re, tw_im = twist_ref[0], twist_ref[1]
    return jnp.concatenate([real * tw_re - imag * tw_im, real * tw_im + imag * tw_re], 1)


def turned_back(second, twist_ref):
    imag, real = second[:, :HALF], second[:, HALF:]
    tw_re, tw_im = twist_ref[0], twist_ref[1]
    parts = [real * tw_re + imag * tw_im, imag * tw_re - real * tw_im]
    return jnp.stack([part.reshape(-1, RUN, HALF) for part in parts], 1).reshape(-1, HALF)


def sequences_kernel(undo, recv_ref, lead_ref, back_ref, trail_ref, twist_ref, spec_ref, part_ref, cross):
    n_ctx, n_slab = recv_ref.shape[:2]
    rows = 2 * n_ctx * GROUP
    pair = 2 * GROUP

    parts = []
    for group in (0, 1):
        for slab in range(n_slab):
            both = [
                recv_ref[:, slab, k * 2 * pair + group * pair : k * 2 * pair + (group + 1) * pair]
                for k in (0, 1)
            ]
            first = dot(lead_ref[...], jnp.concatenate([part.reshape(rows, HALF) for part in both], 1))
            spec_in = dot(turned(first[:, :HALF], twist_ref).astype(BF16), trail_ref[...])
            spec_grad = dot(turned(first[:, HALF:], twist_ref).astype(BF16), trail_ref[...])
            spec_ref[2 * slab + group] = spec_grad
            in_re, in_im = spec_in[:, :HALF], spec_in[:, HALF:]
            grad_re, grad_im = spec_grad[:, :HALF], spec_grad[:, HALF:]
            cross_im = in_re * grad_im - in_im * grad_re
            cross_re = in_re * grad_re + in_im * grad_im
            if slab == 0:
                cross[group, :, :HALF] = cross_im
                cross[group, :, HALF:] = cross_re
            else:
                cross[group, :, :HALF] += cross_im
                cross[group, :, HALF:] += cross_re

        high, low = split(cross[group])
        second = dot(high, trail_ref[...]) + dot(low, trail_ref[...])
        parts.append(turned_back(second, twist_ref).astype(BF16))
    result = dot(back_ref[...], jnp.concatenate(parts, 1)) * undo
    for group in (0, 1):
        part = result[:, group * HALF : (group + 1) * HALF].astype(BF16)
        part_ref[:, group * pair : (group + 1) * pair] = part.reshape(n_ctx, pair, HALF)


def inverse_kernel(undo, own_ref, other_ref, spec_ref, lead_ref, back_ref, trail_ref, twist_ref, out_ref):
    n_ctx = own_ref.shape[0]
    n_slab = out_ref.shape[1]
    rows = 2 * n_ctx * GROUP
    pair = 2 * GROUP
    core = lax.axis_index("core")

    both = [ref[...].reshape(rows, HALF) for ref in (own_ref, other_ref)]
    first = dot(lead_ref[...], jnp.concatenate(both, 1))
    parts = [[] for _ in range(n_slab)]
    for k, group in ((0, core), (1, 1 - core)):
        filt = dot(turned(first[:, k * HALF : (k + 1) * HALF], twist_ref).astype(BF16), trail_ref[...]) * undo
        filt_re, filt_im = filt[:, :HALF], filt[:, HALF:]
        for slab in range(n_slab):
            grad_re, grad_im = spec_ref[2 * slab + group, :, :HALF], spec_ref[2 * slab + group, :, HALF:]
            back_re = filt_re * grad_re + filt_im * grad_im
            back_im = filt_re * grad_im - filt_im * grad_re
            product = jnp.concatenate([back_im, back_re], 1).astype(BF16)
            parts[slab].append(turned_back(dot(product, trail_ref[...]), twist_ref).astype(BF16))
    for slab in range(n_slab):
        result = dot(back_ref[...], jnp.concatenate(parts[slab], 1))
        for k, group in ((0, core), (1, 1 - core)):
            part = result[:, k * HALF : (k + 1) * HALF].astype(BF16)
            out_ref[:, slab, pl.ds(pl.multiple_of(group * pair, pair), pair)] = part.reshape(n_ctx, pair, HALF)


def sum_kernel(mine_ref, other_ref, din_ref, out_ref):
    n_ctx = mine_ref.shape[0]
    pair = 2 * GROUP
    core = lax.axis_index("core")
    total = mine_ref[...].astype(F32) + other_ref[...].astype(F32)
    lane = lax.broadcasted_iota(jnp.int32, (n_ctx * GROUP, HALF), 1)
    out_ref[:, :, : 2 * pair] = din_ref[...]
    for h in (0, 1):
        first, second = [
            total[:, group * pair + h * GROUP : group * pair + (h + 1) * GROUP].reshape(n_ctx * GROUP, HALF)
            for group in (0, 1)
        ]
        first = jnp.where(core == 0, first, pltpu.roll(first, HALF // 2, 1))
        second = jnp.where(core == 0, pltpu.roll(second, HALF // 2, 1), second)
        both = jnp.where(lane < HALF // 2, first, second)
        out_ref[:, h, 2 * pair :] = both.reshape(n_ctx, GROUP, HALF).astype(BF16)


def packed(inputs, grad_out, filters, core, y_hi):
    def tiles(values):
        split_up = values.reshape(-1, 2, GROUP, 2, HALF).transpose(0, 1, 3, 2, 4)
        return split_up.reshape(-1, 4, GROUP, HALF)

    none = (0, 0, 0)

    def placed(values, low, high):
        return lax.pad(tiles(values), jnp.zeros((), BF16), (none, (low, high, 0), none, none))

    tile = lax.broadcasted_iota(jnp.int32, (1, 9, 1, 1), 1)
    last = placed(filters, 8, 0)
    last = lax.dynamic_slice_in_dim(last, 2 * core + y_hi, 9, axis=1)
    return jnp.where(tile < 4, placed(inputs, 0, 5), jnp.where(tile < 8, placed(grad_out, 4, 1), last))


def per_device(inputs, grad_out, filters):
    n_ctx, n_slab = lax.axis_size("ctx"), lax.axis_size("y_hi")
    rows = 2 * n_ctx * GROUP
    lead, back, trail, twist, undo = make_tables(2 * n_ctx)
    lead, back, trail, twist = [jnp.asarray(table) for table in (lead, back, trail, twist)]
    vmem = pl.BlockSpec(memory_space=pltpu.VMEM)
    spectra = pltpu.VMEM((2, rows, 2 * HALF), F32)

    def kernel(body, name, operands, out_shape, scratch, flops):
        several = isinstance(out_shape, tuple)
        return pl.pallas_call(
            body,
            in_specs=[vmem] * len(operands),
            out_specs=tuple(vmem for _ in out_shape) if several else vmem,
            out_shape=out_shape,
            scratch_shapes=scratch,
            compiler_params=pltpu.CompilerParams(vmem_limit_bytes=40 * 2**20),
            cost_estimate=pl.CostEstimate(flops=flops, bytes_accessed=2**21, transcendentals=0),
            name=name,
        )(*operands)

    def exchange(blocks):
        return lax.all_to_all(blocks, ("ctx", "y_hi"), split_axis=0, concat_axis=0)

    def swapped(values):
        return lax.ppermute(values, "core", ((0, 1), (1, 0)))

    def shape(*sizes, dtype=BF16):
        return jax.ShapeDtypeStruct(sizes, dtype)

    received = exchange(packed(inputs[0], grad_out[0], filters, lax.axis_index("core"), lax.axis_index("y_hi")))
    own = received[:, 8].reshape(n_ctx, 2 * GROUP, HALF)
    other = swapped(own)
    received = received.reshape(n_ctx, n_slab, 9 * GROUP, HALF)
    spec_grad, mine = kernel(
        functools.partial(sequences_kernel, undo),
        "sequences",
        (received, lead, back, trail, twist),
        (shape(2 * n_slab, rows, 2 * HALF, dtype=F32), shape(n_ctx, 4 * GROUP, HALF)),
        [spectra],
        4 * 10**9,
    )
    theirs = swapped(mine)
    din = kernel(
        functools.partial(inverse_kernel, undo),
        "inverse",
        (own, other, spec_grad, lead, back, trail, twist),
        shape(n_ctx, n_slab, 4 * GROUP, HALF),
        [],
        3 * 10**9,
    )
    returned = kernel(sum_kernel, "sum", (mine, theirs, din), shape(n_ctx, n_slab, 5 * GROUP, HALF), [], 10**6)
    returned = exchange(returned.reshape(n_ctx * n_slab, 5, GROUP, HALF))
    dinputs = returned[:, :4].reshape(-1, 2, 2, GROUP, HALF).transpose(0, 1, 3, 2, 4).reshape(inputs.shape)
    side = jnp.asarray(np.repeat(np.eye(2), HALF // 2, axis=1).reshape(1, 2, 1, HALF) > 0)
    both = jnp.where(side, returned[:, 4][:, None], jnp.zeros((), BF16)).reshape(-1, HALF)
    eye = np.eye(HALF // 2)
    pick = jnp.asarray(np.concatenate([eye, eye], 1).astype(ml_dtypes.bfloat16))
    dfilters = lax.dot_general(pick, both, (((1,), (1,)), ((), ())), preferred_element_type=F32)
    return dinputs, dfilters.T


def solution(mesh):
    n_ctx, n_ch = mesh.devices.shape
    fine = Mesh(mesh.devices.reshape(n_ctx, n_ch // 2, 2), ("ctx", "y_hi", "core"))
    channels = ("y_hi", "core")
    placed = (P(None, channels, "ctx"), P(None, channels, "ctx"), P(None, "ctx"))
    return jax.shard_map(
        per_device,
        mesh=fine,
        in_specs=placed,
        out_specs=(P(None, channels, "ctx"), P(None, ("ctx",) + channels)),
        check_vma=False,
    )
```
